512 devices in a mesh: case: 8 (over x, core), slab: 64 (over y, z).
Axes of the slice: x: 4, y: 4, z: 16, core: 2. Of those that a mesh axis runs over, the one named last changes fastest.
Arguments:
- sensitivity: float32 [8, 8388608], P('case', 'slab'), may hold values from -300 to 300
- material_share_now: float32 [64, 8, 16384], P('slab', 'case'), may hold values from 0.05 to 0.95
- material_share_prior: float32 [64, 8, 16384], P('slab', 'case'), may hold values from 0.05 to 0.95
- material_share_prior_prior: float32 [64, 8, 16384], P('slab', 'case'), may hold values from 0.05 to 0.95
- floor_asym_gap: float32 [64, 8, 16384], P('slab', 'case'), may hold values from 0.005 to 0.5
- ceiling_asym_gap: float32 [64, 8, 16384], P('slab', 'case'), may hold values from 0.005 to 0.5
- volume_weight: float32 [64, 8, 16384], P('slab', 'case'), may hold values from 0.5 to 2
- case_values: float32 [8], replicated, may hold values from 0.5 to 1.5
- duals_start: float32 [9], replicated, may hold values from 0.05 to 0.5
Outputs:
- new_design: float32 [64, 8, 16384], P('slab', 'case')
- lower_asym: float32 [64, 8, 16384], P('slab', 'case')
- upper_asym: float32 [64, 8, 16384], P('slab', 'case')
- duals: float32 [9], replicated
The draws below stay inside these ranges and needn't reach their ends.
All inputs are finite; a program needn't handle non-finite values.
Results may differ from the reference program's by a relative error of at most 0.0003.
Values sent between devices are 32-bit elements; how exact they have to be, the bound alone decides.
No kernel may reach another device: no remote copies, remote signals or barrier semaphores. Data moves between devices by JAX's collectives and lax.ppermute only.
A program may use at most 64 MiB of HBM per device.

```python
import math
from functools import partial
import jax
import jax.numpy as jnp
from jax import lax

CASES = 8
NEWTON = 4
EL_DEV = 16384
DUALS = 9
NEL = 8388608
N_CASE = 8
N_SLAB = 64


def draw_sensitivity(key, part):
    key = jax.random.fold_in(key, 11)
    keys = jax.random.split(key, 3)
    elements = jnp.arange(NEL).astype(jnp.float32)
    ramp = 1.0 + 2.0 * elements / (NEL - 1)
    case_scale = jnp.exp(jax.random.uniform(keys[1], (CASES, 1)) * math.log(10.0))
    element_scale = jnp.exp(jax.random.uniform(keys[0], (1, NEL)) * math.log(10.0))
    spread = jax.random.truncated_normal(keys[2], -4.0, 4.0, (CASES, NEL))
    mixed = -0.8 + 0.6 * spread
    scale_factor = 0.3
    return (scale_factor * mixed * ramp[None, :] * element_scale * case_scale).astype(jnp.float32)


def shard_levels(own_key, extent, cuts, least, high):
    def one(position, shards_of):
        steps = jax.random.uniform(jax.random.fold_in(jax.random.fold_in(own_key, 6), position), (shards_of,), jnp.float32, least / len(cuts), high / len(cuts))
        return jnp.repeat(jnp.exp(steps), extent[position] // shards_of).reshape((-1,) + (1,) * (len(extent) - position - 1))

    factor_of = one(*cuts[0])
    for cut in cuts[1:]:
        factor_of = factor_of * one(*cut)
    return factor_of


def setup_inputs(seed: int = 0) -> dict:
    key_of = jax.random.split(jax.random.key(seed), 10)
    sensitivity = draw_sensitivity(jax.random.fold_in(key_of[9], 71), 0)
    material_share_now = jnp.clip(0.05 + 0.9 * jax.random.uniform(key_of[1], (N_SLAB, N_CASE, EL_DEV), jnp.float32) ** shard_levels(key_of[1], (N_SLAB, N_CASE, EL_DEV), ((0, 64), (1, 8)), -0.2, 0.2), 0.05, 0.95)
    material_share_prior = jnp.clip(0.05 + 0.9 * jax.random.uniform(key_of[2], (N_SLAB, N_CASE, EL_DEV), jnp.float32) ** shard_levels(key_of[2], (N_SLAB, N_CASE, EL_DEV), ((0, 64), (1, 8)), -0.2, 0.2), 0.05, 0.95)
    material_share_prior_prior = jnp.clip(0.05 + 0.9 * jax.random.uniform(key_of[3], (N_SLAB, N_CASE, EL_DEV), jnp.float32) ** shard_levels(key_of[3], (N_SLAB, N_CASE, EL_DEV), ((0, 64), (1, 8)), -0.2, 0.2), 0.05, 0.95)
    floor_asym_gap = jnp.clip(jnp.exp(math.log(0.5) - 4.6051702 * jax.random.uniform(key_of[4], (N_SLAB, N_CASE, EL_DEV), jnp.float32) ** shard_levels(key_of[4], (N_SLAB, N_CASE, EL_DEV), ((0, 64), (1, 8)), -0.2, 0.2)), 0.005, 0.5)
    ceiling_asym_gap = jnp.clip(jnp.exp(math.log(0.5) - 4.6051702 * jax.random.uniform(key_of[5], (N_SLAB, N_CASE, EL_DEV), jnp.float32) ** shard_levels(key_of[5], (N_SLAB, N_CASE, EL_DEV), ((0, 64), (1, 8)), -0.2, 0.2)), 0.005, 0.5)
    volume_weight = jnp.clip(jnp.exp(math.log(2.0) - 1.3862944 * jax.random.uniform(key_of[6], (N_SLAB, N_CASE, EL_DEV), jnp.float32) ** shard_levels(key_of[6], (N_SLAB, N_CASE, EL_DEV), ((0, 64), (1, 8)), -0.2, 0.2)), 0.5, 2.0)
    case_values = jnp.clip(jax.random.uniform(key_of[7], (CASES,), jnp.float32, 0.5, 1.5), 0.5, 1.5)
    duals_start = jnp.clip(jnp.exp(jax.random.uniform(key_of[8], (DUALS,), jnp.float32, math.log(0.05), math.log(0.5))), 0.05, 0.5)
    return {"sensitivity": sensitivity, "material_share_now": material_share_now, "material_share_prior": material_share_prior, "material_share_prior_prior": material_share_prior_prior, "floor_asym_gap": floor_asym_gap, "ceiling_asym_gap": ceiling_asym_gap, "volume_weight": volume_weight, "case_values": case_values, "duals_start": duals_start}


PROX = 0.1
VOLFRAC = 0.4

def limit_couple(material_share_now, material_share_prior, material_share_prior_prior, floor_asym_gap, ceiling_asym_gap):
    trend = (material_share_now - material_share_prior) * (material_share_prior - material_share_prior_prior)
    factor = jnp.where(trend > 0, 1.2, jnp.where(trend < 0, 0.7, 1.0)).astype(material_share_now.dtype)
    minimal_limit = jnp.minimum(material_share_now - factor * floor_asym_gap, material_share_now - 0.01)
    maximal_limit = jnp.maximum(material_share_now + factor * ceiling_asym_gap, material_share_now + 0.01)
    return (minimal_limit, maximal_limit)

def bounds(material_share_now, minimal_limit, maximal_limit):
    floor_x = jnp.maximum(jnp.maximum(minimal_limit + 0.1 * (material_share_now - minimal_limit), material_share_now - 0.2), 0.0)
    ceil_x = jnp.minimum(jnp.minimum(maximal_limit - 0.1 * (maximal_limit - material_share_now), material_share_now + 0.2), 1.0)
    above = (maximal_limit - material_share_now) ** 2
    below = (material_share_now - minimal_limit) ** 2
    return (floor_x, ceil_x, above, below)

def weighted(material_share_now, minimal_limit, maximal_limit, above, below, slopes):
    rising = jnp.maximum(slopes, 0.0)
    falling = jnp.maximum(-slopes, 0.0)
    upward = above * (1.001 * rising + 0.001 * falling)
    downward = below * (0.001 * rising + 1.001 * falling)
    at_start = upward / (maximal_limit - material_share_now) + downward / (material_share_now - minimal_limit)
    return (upward, downward, at_start)

def prepare(material_share_now, material_share_prior, material_share_prior_prior, floor_asym_gap, ceiling_asym_gap, slopes):
    minimal_limit, maximal_limit = limit_couple(material_share_now, material_share_prior, material_share_prior_prior, floor_asym_gap, ceiling_asym_gap)
    floor_x, ceil_x, above, below = bounds(material_share_now, minimal_limit, maximal_limit)
    upward, downward, at_start = weighted(material_share_now, minimal_limit, maximal_limit, above, below, slopes)
    return (minimal_limit, maximal_limit, floor_x, ceil_x, above, below, upward, downward, at_start)

def place(big_p, big_q, minimal_limit, maximal_limit, floor_x, ceil_x):
    root_p = jnp.sqrt(big_p)
    root_q = jnp.sqrt(big_q)
    free_x = (root_p * minimal_limit + root_q * maximal_limit) / (root_p + root_q)
    chosen = jnp.minimum(jnp.maximum(free_x, floor_x), ceil_x)
    inside = jnp.where((free_x > floor_x) & (free_x < ceil_x), 1.0, 0.0).astype(free_x.dtype)
    return (chosen, inside)

def measure(upward, downward, chosen, inside, big_p, big_q, minimal_limit, maximal_limit):
    to_upper = maximal_limit - chosen
    to_lower = chosen - minimal_limit
    values = upward / to_upper + downward / to_lower
    slope = upward / (to_upper * to_upper) - downward / (to_lower * to_lower)
    curve = 2.0 * big_p / to_upper ** 3 + 2.0 * big_q / to_lower ** 3
    scaled = slope * jnp.sqrt(inside / curve)
    return (values, scaled)

def solve_small(matrix, vector):
    dual_count = vector.shape[0]
    factor_l = jnp.linalg.cholesky(matrix)
    forward = []
    for row_at in range(dual_count):
        running = vector[row_at]
        for col_at in range(row_at):
            running = running - factor_l[row_at, col_at] * forward[col_at]
        forward.append(running / factor_l[row_at, row_at])
    backward = [None] * dual_count
    for row_at in reversed(range(dual_count)):
        running = forward[row_at]
        for col_at in range(row_at + 1, dual_count):
            running = running - factor_l[col_at, row_at] * backward[col_at]
        backward[row_at] = running / factor_l[row_at, row_at]
    return jnp.stack(backward)

def advance(duals, grad_total, hess_total, case_values, element_total):
    dual_count = duals.shape[0]
    coupling = jnp.concatenate([jnp.ones((dual_count - 1,), duals.dtype), jnp.zeros((1,), duals.dtype)])
    excess = jnp.sum(duals[:-1]) - 1.0
    height = jnp.maximum(excess, 0.0)
    active = jnp.where(excess > 0, 1.0, 0.0).astype(duals.dtype)
    target = jnp.concatenate([case_values, jnp.full((1,), -VOLFRAC, duals.dtype)])
    gradient = grad_total / element_total + target - coupling * height
    negative = hess_total / element_total + coupling[:, None] * coupling[None, :] * active
    damping = 0.5 * jnp.trace(negative) / dual_count + 0.0001
    matrix = negative + damping * jnp.eye(dual_count, dtype=duals.dtype)
    step_dual = solve_small(matrix, gradient)
    return jnp.maximum(duals + step_dual, 0.1 * duals)

def block_terms(duals, block):
    sens_block, material_share_now, material_share_prior, material_share_prior_prior, floor_asym_gap, ceiling_asym_gap, weight = block
    slopes = jnp.concatenate([sens_block, weight[None]], 0)
    minimal_limit, maximal_limit, floor_x, ceil_x, above, below, upward, downward, at_start = prepare(material_share_now, material_share_prior, material_share_prior_prior, floor_asym_gap, ceiling_asym_gap, slopes)
    big_p = PROX * above + jnp.dot(duals, upward, precision=lax.Precision.HIGHEST)
    big_q = PROX * below + jnp.dot(duals, downward, precision=lax.Precision.HIGHEST)
    chosen, inside = place(big_p, big_q, minimal_limit, maximal_limit, floor_x, ceil_x)
    values, scaled = measure(upward, downward, chosen, inside, big_p, big_q, minimal_limit, maximal_limit)
    hessian = jnp.dot(scaled, scaled.T, precision=lax.Precision.HIGHEST)
    return (lax.optimization_barrier(jnp.sum(values, 1)), hessian, chosen, minimal_limit, maximal_limit)

def start_block(block):
    sens_block, material_share_now, material_share_prior, material_share_prior_prior, floor_asym_gap, ceiling_asym_gap, weight = block
    slopes = jnp.concatenate([sens_block, weight[None]], 0)
    prepared = prepare(material_share_now, material_share_prior, material_share_prior_prior, floor_asym_gap, ceiling_asym_gap, slopes)
    return (lax.optimization_barrier(jnp.sum(prepared[8], 1)), jnp.sum(weight * material_share_now))

def reference(sensitivity, material_share_now, material_share_prior, material_share_prior_prior, floor_asym_gap, ceiling_asym_gap, volume_weight, case_values, duals_start):
    blocks = material_share_now.shape[0]
    per_block = sensitivity.shape[1] // blocks
    sens_blocks = jnp.transpose(sensitivity.reshape(sensitivity.shape[0], blocks, per_block), (1, 0, 2))

    def flatten(array):
        return array.reshape(blocks, per_block)
    stacked = (sens_blocks, flatten(material_share_now), flatten(material_share_prior), flatten(material_share_prior_prior), flatten(floor_asym_gap), flatten(ceiling_asym_gap), flatten(volume_weight))
    start_sums, volume_sums = lax.map(start_block, stacked)
    dual_count = duals_start.shape[0]
    offset = -lax.optimization_barrier(jnp.sum(start_sums, 0)) + jnp.concatenate([jnp.zeros((dual_count - 1,), duals_start.dtype), jnp.sum(volume_sums)[None]])
    element_total = jnp.asarray(sensitivity.shape[1], duals_start.dtype)
    duals = duals_start
    for newton_step in range(NEWTON):
        results = lax.map(partial(block_terms, duals), stacked)
        duals = advance(duals, lax.optimization_barrier(jnp.sum(results[0], 0)) + offset, lax.optimization_barrier(jnp.sum(results[1], 0)), case_values, element_total)
    results = lax.map(partial(block_terms, duals), stacked)
    shape = material_share_now.shape
    return (results[2].reshape(shape), results[3].reshape(shape), results[4].reshape(shape), duals)
```

```python
import functools

import jax
import jax.numpy as jnp
from jax import lax
from jax.experimental import pallas as pl
from jax.experimental.pallas import tpu as pltpu
from jax.sharding import Mesh
from jax.sharding import PartitionSpec as P

NEWTON = 4
PROX = 0.1
VOLFRAC = 0.4
N = 9
PAIRS = [(i, k) for i in range(N) for k in range(i + 1)]
GRAD_AT = len(PAIRS)
VOL_AT = GRAD_AT + N
LANES = 128
HIGHEST = lax.Precision.HIGHEST


def vmem():
    return pl.BlockSpec(memory_space=pltpu.VMEM)


def smem():
    return pl.BlockSpec(memory_space=pltpu.SMEM)


def total(rows):
    while rows.shape[0] > 8:
        half = rows.shape[0] // 2
        rows = rows[:half] + rows[half:]
    return jnp.sum(rows, 0, keepdims=True)


def spread(gathered, table_ref):
    sums = total(gathered)
    count = table_ref.shape[0]
    row = lax.broadcasted_iota(jnp.int32, (count, LANES), 0)
    lane = lax.broadcasted_iota(jnp.int32, (count, LANES), 1)
    diagonal = jnp.where(row == lane, sums, 0.0)
    table_ref[...] = jnp.dot(
        diagonal,
        jnp.ones((LANES, LANES), jnp.float32),
        precision=HIGHEST,
        preferred_element_type=jnp.float32,
    )


def solve(matrix, vector):
    m = dict(matrix)
    b = list(vector)
    inverse = []
    for k in range(N):
        r = 1.0 / m[k, k]
        inverse.append(r)
        for i in range(k + 1, N):
            scaled = m[i, k] * r
            for j in range(k + 1, i + 1):
                m[i, j] = m[i, j] - scaled * m[j, k]
            b[i] = b[i] - scaled * b[k]
    x = [None] * N
    for k in reversed(range(N)):
        running = b[k]
        for i in range(k + 1, N):
            running = running - m[i, k] * x[i]
        x[k] = running * inverse[k]
    return x


def newton(table_ref, duals, volume, case_values_ref, element_total):
    scale = 1.0 / element_total
    excess = functools.reduce(jnp.add, duals[:-1]) - 1.0
    height = jnp.maximum(excess, 0.0)
    active = jnp.where(excess > 0, 1.0, 0.0)
    matrix = {}
    for at, (i, k) in enumerate(PAIRS):
        entry = table_ref[at : at + 1, :] * scale
        if i < N - 1:
            entry = entry + active
        matrix[i, k] = entry
    trace = functools.reduce(jnp.add, [matrix[i, i] for i in range(N)])
    damping = trace * (0.5 / N) + 0.0001
    vector = []
    for i in range(N):
        matrix[i, i] = matrix[i, i] + damping
        entry = table_ref[GRAD_AT + i : GRAD_AT + i + 1, :] * scale
        if i < N - 1:
            entry = entry + case_values_ref[i] - height
        else:
            entry = entry + volume - VOLFRAC
        vector.append(entry)
    step = solve(matrix, vector)
    return [jnp.maximum(l + d, 0.1 * l) for l, d in zip(duals, step)]


def place(duals, ups, downs, a, b, lo, hi):
    p = functools.reduce(jnp.add, [l * u for l, u in zip(duals, ups)]) + PROX
    q = functools.reduce(jnp.add, [l * d for l, d in zip(duals, downs)]) + PROX
    root_p = jnp.sqrt(p)
    root_q = jnp.sqrt(q)
    free = a * b * (root_q - root_p) / (a * root_p + b * root_q)
    return p, q, free, jnp.minimum(jnp.maximum(free, lo), hi)


def evaluate(duals, up_ref, down_ref, aux_ref, scaled_ref, stat_ref):
    steps = aux_ref.shape[1] // 8
    duals = [jnp.broadcast_to(l, (8, LANES)) for l in duals]

    def column(j, grads):
        rows = pl.ds(pl.multiple_of(j * 8, 8), 8)
        a, b, lo, hi = (aux_ref[k, rows, :] for k in range(4))
        ups = [up_ref[i, rows, :] for i in range(N)]
        downs = [down_ref[i, rows, :] for i in range(N)]
        p, q, free, t = place(duals, ups, downs, a, b, lo, hi)
        inside = (free > lo) & (free < hi)
        ru = 1.0 / (a - t)
        rl = 1.0 / (b + t)
        up_at = a * ru
        down_at = b * rl
        up_two = up_at * up_at
        down_two = down_at * down_at
        curve = 2.0 * (p * up_two * ru + q * down_two * rl)
        root = jnp.where(inside, lax.rsqrt(curve), 0.0)
        cu, cd = up_two * root, down_two * root
        tu, td = t * up_at, t * down_at
        out = []
        for i in range(N):
            scaled_ref[i, rows, :] = cu * ups[i] - cd * downs[i]
            out.append(grads[i] + (tu * ups[i] - td * downs[i]))
        return tuple(out)

    zero = jnp.zeros((8, LANES), jnp.float32)
    grads = lax.fori_loop(0, steps, column, (zero,) * N)
    for i in range(N):
        stat_ref[GRAD_AT + i : GRAD_AT + i + 1, :] = jnp.sum(grads[i], 0, keepdims=True)
    groups = [(0, 3), (3, 6), (6, 9)]
    for at, (i0, i1) in enumerate(groups):
        for k0, k1 in groups[: at + 1]:
            pairs = [(i, k) for i in range(i0, i1) for k in range(k0, min(k1, i + 1))]

            def products(j, sums, pairs=pairs):
                rows = pl.ds(pl.multiple_of(j * 8, 8), 8)
                held = {i: scaled_ref[i, rows, :] for i in sorted({i for pair in pairs for i in pair})}
                return tuple(s + held[i] * held[k] for s, (i, k) in zip(sums, pairs))

            sums = lax.fori_loop(0, steps, products, (zero,) * len(pairs), unroll=4)
            for s, pair in zip(sums, pairs):
                row = PAIRS.index(pair)
                stat_ref[row : row + 1, :] = jnp.sum(s, 0, keepdims=True)


def announce(stat_ref, message_ref):
    sums = lax.dot_general(
        jnp.ones((8, LANES), jnp.float32),
        stat_ref[...],
        (((1,), (1,)), ((), ())),
        precision=HIGHEST,
        preferred_element_type=jnp.float32,
    )
    for at in range(0, message_ref.shape[0], 8):
        message_ref[at : at + 8, :] = sums


def first_kernel(
    duals_ref, g_ref, x_ref, x1_ref, x2_ref, gl_ref, gu_ref, w_ref,
    lower_ref, upper_ref, up_ref, down_ref, aux_ref, state_ref, message_ref,
    scaled_ref, stat_ref,
):
    steps = x_ref.shape[0] // 8

    def column(j, volume):
        rows = pl.ds(pl.multiple_of(j * 8, 8), 8)
        x, x1, x2, w = (r[rows, :] for r in (x_ref, x1_ref, x2_ref, w_ref))
        trend = (x - x1) * (x1 - x2)
        factor = jnp.where(trend > 0, 1.2, jnp.where(trend < 0, 0.7, 1.0))
        lower = jnp.minimum(x - factor * gl_ref[rows, :], x - 0.01)
        upper = jnp.maximum(x + factor * gu_ref[rows, :], x + 0.01)
        lower_ref[rows, :] = lower
        upper_ref[rows, :] = upper
        a = upper - x
        b = x - lower
        aux_ref[0, rows, :] = a
        aux_ref[1, rows, :] = b
        aux_ref[2, rows, :] = jnp.maximum(jnp.maximum(lower + 0.1 * b, x - 0.2), 0.0) - x
        aux_ref[3, rows, :] = jnp.minimum(jnp.minimum(upper - 0.1 * a, x + 0.2), 1.0) - x
        for i in range(N):
            g = g_ref[i, rows, :] if i < N - 1 else w
            up_ref[i, rows, :] = jnp.maximum(1.001 * g, -0.001 * g)
            down_ref[i, rows, :] = jnp.maximum(0.001 * g, -1.001 * g)
        return volume + w * x

    volume = lax.fori_loop(0, steps, column, jnp.zeros((8, LANES), jnp.float32))
    stat_ref[VOL_AT:, :] = jnp.zeros((LANES - VOL_AT, LANES), jnp.float32)
    stat_ref[VOL_AT : VOL_AT + 1, :] = jnp.sum(volume, 0, keepdims=True)
    duals = [jnp.full((1, LANES), duals_ref[i], jnp.float32) for i in range(N)]
    state_ref[...] = jnp.zeros(state_ref.shape, jnp.float32)
    for i in range(N):
        state_ref[i : i + 1, :] = duals[i]
    evaluate(duals, up_ref, down_ref, aux_ref, scaled_ref, stat_ref)
    announce(stat_ref, message_ref)


def update(element_total, case_values_ref, gathered_ref, state_ref, table_ref):
    spread(gathered_ref[...], table_ref)
    duals = [state_ref[i : i + 1, :] for i in range(N)]
    volume = state_ref[N : N + 1, :] + table_ref[VOL_AT : VOL_AT + 1, :] * (1.0 / element_total)
    return newton(table_ref, duals, volume, case_values_ref, element_total), volume


def middle_kernel(
    element_total,
    case_values_ref, gathered_ref, state_ref, up_ref, down_ref, aux_ref,
    new_state_ref, message_ref,
    scaled_ref, stat_ref, table_ref,
):
    duals, volume = update(element_total, case_values_ref, gathered_ref, state_ref, table_ref)
    new_state_ref[...] = jnp.zeros(new_state_ref.shape, jnp.float32)
    for i in range(N):
        new_state_ref[i : i + 1, :] = duals[i]
    new_state_ref[N : N + 1, :] = volume
    stat_ref[VOL_AT:, :] = jnp.zeros((LANES - VOL_AT, LANES), jnp.float32)
    evaluate(duals, up_ref, down_ref, aux_ref, scaled_ref, stat_ref)
    announce(stat_ref, message_ref)


def last_kernel(
    element_total,
    case_values_ref, gathered_ref, state_ref, up_ref, down_ref, aux_ref, x_ref,
    design_ref, duals_ref,
    table_ref,
):
    duals, _ = update(element_total, case_values_ref, gathered_ref, state_ref, table_ref)
    lane = lax.broadcasted_iota(jnp.int32, (1, LANES), 1)
    row = jnp.zeros((1, LANES), jnp.float32)
    for i in range(N):
        row = jnp.where(lane == i, duals[i], row)
    duals_ref[...] = row
    wide = [jnp.broadcast_to(l, (8, LANES)) for l in duals]

    def column(j, carry):
        rows = pl.ds(pl.multiple_of(j * 8, 8), 8)
        a, b, lo, hi = (aux_ref[k, rows, :] for k in range(4))
        ups = [up_ref[i, rows, :] for i in range(N)]
        downs = [down_ref[i, rows, :] for i in range(N)]
        _, _, _, t = place(wide, ups, downs, a, b, lo, hi)
        design_ref[rows, :] = x_ref[rows, :] + t
        return carry

    lax.fori_loop(0, aux_ref.shape[1] // 8, column, 0)


def f32(*shape):
    return jax.ShapeDtypeStruct(shape, jnp.float32)


PARAMS = pltpu.CompilerParams(vmem_limit_bytes=16 * 1024 * 1024)
NEAR = ("x", "y")
FAR = ("core", "z")


def per_device(sensitivity, x, x1, x2, gl, gu, w, case_values, duals_start):
    sizes = {name: lax.axis_size(name) for name in ("x", "core", "y", "z")}
    near = sizes["x"] * sizes["y"]
    far = sizes["core"] * sizes["z"]
    cases = sizes["x"] * sizes["core"]
    depth = x.size // LANES
    element_total = float(x.size * near * far)
    shape = x.shape
    x, x1, x2, gl, gu, w = (v.reshape(depth, LANES) for v in (x, x1, x2, gl, gu, w))
    g = lax.all_to_all(
        sensitivity.reshape(cases, depth, LANES), ("x", "core"), split_axis=0, concat_axis=0, tiled=True
    )

    def gather(message):
        heard = lax.all_to_all(message, NEAR, split_axis=0, concat_axis=0, tiled=True)
        part = jnp.broadcast_to(jnp.sum(heard, 0, keepdims=True), (far, LANES))
        return lax.all_to_all(part, FAR, split_axis=0, concat_axis=0, tiled=True)

    lower, upper, up, down, aux, state, message = pl.pallas_call(
        first_kernel,
        out_shape=(
            f32(depth, LANES), f32(depth, LANES), f32(N, depth, LANES), f32(N, depth, LANES),
            f32(4, depth, LANES), f32(16, LANES), f32(near, LANES),
        ),
        in_specs=[smem()] + [vmem()] * 7,
        out_specs=(vmem(),) * 7,
        scratch_shapes=[pltpu.VMEM((N, depth, LANES), jnp.float32), pltpu.VMEM((LANES, LANES), jnp.float32)],
        compiler_params=PARAMS,
    )(duals_start, g, x, x1, x2, gl, gu, w)
    for _ in range(NEWTON - 1):
        state, message = pl.pallas_call(
            functools.partial(middle_kernel, element_total),
            out_shape=(f32(16, LANES), f32(near, LANES)),
            in_specs=[smem()] + [vmem()] * 5,
            out_specs=(vmem(),) * 2,
            scratch_shapes=[
                pltpu.VMEM((N, depth, LANES), jnp.float32),
                pltpu.VMEM((LANES, LANES), jnp.float32),
                pltpu.VMEM((64, LANES), jnp.float32),
            ],
            compiler_params=PARAMS,
        )(case_values, gather(message), state, up, down, aux)
    design, duals = pl.pallas_call(
        functools.partial(last_kernel, element_total),
        out_shape=(f32(depth, LANES), f32(1, LANES)),
        in_specs=[smem()] + [vmem()] * 6,
        out_specs=(vmem(),) * 2,
        scratch_shapes=[pltpu.VMEM((64, LANES), jnp.float32)],
        compiler_params=PARAMS,
    )(case_values, gather(message), state, up, down, aux, x)
    return design.reshape(shape), lower.reshape(shape), upper.reshape(shape), duals[0, :N]


def solution(mesh):
    cases, slabs = mesh.devices.shape
    fine = Mesh(mesh.devices.reshape(cases // 2, 2, 4, slabs // 4), ("x", "core", "y", "z"))
    case, slab = ("x", "core"), ("y", "z")
    design = P(slab, case, None)
    return jax.shard_map(
        per_device,
        mesh=fine,
        in_specs=(P(case, slab),) + (design,) * 6 + (P(), P()),
        out_specs=(design, design, design, P()),
        check_vma=False,
    )
```

```python
import functools

import jax
import jax.numpy as jnp
from jax import lax
from jax.experimental import pallas as pl
from jax.experimental.pallas import tpu as pltpu
from jax.sharding import Mesh
from jax.sharding import PartitionSpec as P

NEWTON = 4
PROX = 0.1
VOLFRAC = 0.4
N = 9
PAIRS = [(i, k) for i in range(N) for k in range(i + 1)]
GRAD_AT = len(PAIRS)
VOL_AT = GRAD_AT + N
LANES = 128
TARGET_AT = 16
STATE = 32
CHUNK = 32
KUNROLL = 16
HIGHEST = lax.Precision.HIGHEST


def vmem():
    return pl.BlockSpec(memory_space=pltpu.VMEM)


def total(rows):
    while rows.shape[0] > 8:
        half = rows.shape[0] // 2
        rows = rows[:half] + rows[half:]
    return jnp.sum(rows, 0, keepdims=True)


def spread(gathered, table_ref):
    sums = total(gathered)
    count = table_ref.shape[0]
    row = lax.broadcasted_iota(jnp.int32, (count, LANES), 0)
    lane = lax.broadcasted_iota(jnp.int32, (count, LANES), 1)
    diagonal = jnp.where(row == lane, sums, 0.0)
    table_ref[...] = jnp.dot(
        diagonal,
        jnp.ones((LANES, LANES), jnp.float32),
        precision=HIGHEST,
        preferred_element_type=jnp.float32,
    )


def solve(matrix, vector):
    m = dict(matrix)
    b = list(vector)
    inverse = []
    for k in range(N):
        r = 1.0 / m[k, k]
        inverse.append(r)
        for i in range(k + 1, N):
            scaled = m[i, k] * r
            for j in range(k + 1, i + 1):
                m[i, j] = m[i, j] - scaled * m[j, k]
            b[i] = b[i] - scaled * b[k]
    x = [None] * N
    for k in reversed(range(N)):
        running = b[k]
        for i in range(k + 1, N):
            running = running - m[i, k] * x[i]
        x[k] = running * inverse[k]
    return x


def newton(table_ref, duals, targets, element_total):
    scale = 1.0 / element_total
    excess = functools.reduce(jnp.add, duals[:-1]) - 1.0
    height = jnp.maximum(excess, 0.0)
    active = jnp.where(excess > 0, 1.0, 0.0)
    matrix = {}
    for at, (i, k) in enumerate(PAIRS):
        entry = table_ref[at : at + 1, :] * scale
        if i < N - 1:
            entry = entry + active
        matrix[i, k] = entry
    trace = functools.reduce(jnp.add, [matrix[i, i] for i in range(N)])
    damping = trace * (0.5 / N) + 0.0001
    vector = []
    for i in range(N):
        matrix[i, i] = matrix[i, i] + damping
        entry = table_ref[GRAD_AT + i : GRAD_AT + i + 1, :] * scale + targets[i]
        vector.append(entry - height if i < N - 1 else entry)
    step = solve(matrix, vector)
    return [jnp.maximum(l + d, 0.1 * l) for l, d in zip(duals, step)]


def place(duals, ups, downs, a, b, lo, hi):
    p = functools.reduce(jnp.add, [l * u for l, u in zip(duals, ups)]) + PROX
    q = functools.reduce(jnp.add, [l * d for l, d in zip(duals, downs)]) + PROX
    root_p = jnp.sqrt(p)
    root_q = jnp.sqrt(q)
    free = a * b * (root_q - root_p) / (a * root_p + b * root_q)
    return p, q, free, jnp.minimum(jnp.maximum(free, lo), hi)


def evaluate(duals, up_ref, down_ref, aux_ref, scaled_ref, stat_ref, before=None):
    depth = aux_ref.shape[1]
    duals = [jnp.broadcast_to(l, (CHUNK, LANES)) for l in duals]

    def fold(v):
        return jnp.sum(v.reshape(-1, 8, LANES), 0)

    def column(j, grads):
        rows = pl.ds(pl.multiple_of(j * CHUNK, CHUNK), CHUNK)
        if before is not None:
            before(rows)
        a, b, lo, hi = (aux_ref[k, rows, :] for k in range(4))
        ups = [up_ref[i, rows, :] for i in range(N)]
        downs = [down_ref[i, rows, :] for i in range(N)]
        p, q, free, t = place(duals, ups, downs, a, b, lo, hi)
        inside = (free > lo) & (free < hi)
        ru = 1.0 / (a - t)
        rl = 1.0 / (b + t)
        up_at = a * ru
        down_at = b * rl
        up_two = up_at * up_at
        down_two = down_at * down_at
        curve = 2.0 * (p * up_two * ru + q * down_two * rl)
        root = jnp.where(inside, lax.rsqrt(curve), 0.0)
        cu, cd = up_two * root, down_two * root
        tu, td = t * up_at, t * down_at
        out = []
        for i in range(N):
            scaled_ref[i, rows, :] = cu * ups[i] - cd * downs[i]
            out.append(grads[i] + fold(tu * ups[i] - td * downs[i]))
        return tuple(out)

    zero = jnp.zeros((8, LANES), jnp.float32)
    grads = lax.fori_loop(0, depth // CHUNK, column, (zero,) * N)
    for i in range(N):
        stat_ref[GRAD_AT + i : GRAD_AT + i + 1, :] = jnp.sum(grads[i], 0, keepdims=True)
    groups = [(0, 3), (3, 6), (6, 9)]
    for at, (i0, i1) in enumerate(groups):
        for k0, k1 in groups[: at + 1]:
            pairs = [(i, k) for i in range(i0, i1) for k in range(k0, min(k1, i + 1))]

            def products(j, sums, pairs=pairs):
                rows = pl.ds(pl.multiple_of(j * 8, 8), 8)
                held = {i: scaled_ref[i, rows, :] for i in sorted({i for pair in pairs for i in pair})}
                return tuple(s + held[i] * held[k] for s, (i, k) in zip(sums, pairs))

            sums = lax.fori_loop(0, depth // 8, products, (zero,) * len(pairs), unroll=KUNROLL)
            for s, pair in zip(sums, pairs):
                row = PAIRS.index(pair)
                stat_ref[row : row + 1, :] = jnp.sum(s, 0, keepdims=True)


def announce(stat_ref, message_ref):
    sums = lax.dot_general(
        jnp.ones((8, LANES), jnp.float32),
        stat_ref[...],
        (((1,), (1,)), ((), ())),
        precision=HIGHEST,
        preferred_element_type=jnp.float32,
    )
    for at in range(0, message_ref.shape[0], 8):
        message_ref[at : at + 8, :] = sums


def prepare_kernel(
    duals_ref, case_values_ref, x_ref, x1_ref, x2_ref, gl_ref, gu_ref, w_ref,
    lower_ref, upper_ref, aux_ref, volume_ref, state_ref,
):
    x, x1, x2, w = (r[...] for r in (x_ref, x1_ref, x2_ref, w_ref))
    trend = (x - x1) * (x1 - x2)
    factor = jnp.where(trend > 0, 1.2, jnp.where(trend < 0, 0.7, 1.0))
    lower = jnp.minimum(x - factor * gl_ref[...], x - 0.01)
    upper = jnp.maximum(x + factor * gu_ref[...], x + 0.01)
    lower_ref[...] = lower
    upper_ref[...] = upper
    a = upper - x
    b = x - lower
    aux_ref[0] = a
    aux_ref[1] = b
    aux_ref[2] = jnp.maximum(jnp.maximum(lower + 0.1 * b, x - 0.2), 0.0) - x
    aux_ref[3] = jnp.minimum(jnp.minimum(upper - 0.1 * a, x + 0.2), 1.0) - x
    volume_ref[...] = jnp.sum((w * x).reshape(-1, 8, LANES), 0)
    state_ref[...] = jnp.zeros(state_ref.shape, jnp.float32)
    for i in range(N):
        state_ref[i : i + 1, :] = jnp.broadcast_to(duals_ref[0:1, i : i + 1], (1, LANES))
    for i in range(N - 1):
        state_ref[TARGET_AT + i : TARGET_AT + i + 1, :] = jnp.broadcast_to(
            case_values_ref[0:1, i : i + 1], (1, LANES)
        )
    state_ref[TARGET_AT + N - 1 : TARGET_AT + N, :] = jnp.full((1, LANES), -VOLFRAC)


def first_kernel(
    g_ref, w_ref, aux_ref, volume_ref, state_ref,
    up_ref, down_ref, message_ref,
    scaled_ref, stat_ref,
):
    def slopes(rows):
        for i in range(N):
            g = g_ref[i, rows, :] if i < N - 1 else w_ref[rows, :]
            up_ref[i, rows, :] = jnp.maximum(1.001 * g, -0.001 * g)
            down_ref[i, rows, :] = jnp.maximum(0.001 * g, -1.001 * g)

    stat_ref[VOL_AT:, :] = jnp.zeros((LANES - VOL_AT, LANES), jnp.float32)
    stat_ref[VOL_AT : VOL_AT + 1, :] = jnp.sum(volume_ref[...], 0, keepdims=True)
    duals = [state_ref[i : i + 1, :] for i in range(N)]
    evaluate(duals, up_ref, down_ref, aux_ref, scaled_ref, stat_ref, slopes)
    announce(stat_ref, message_ref)


def update(element_total, gathered_ref, state_ref, table_ref):
    spread(gathered_ref[...], table_ref)
    duals = [state_ref[i : i + 1, :] for i in range(N)]
    targets = [state_ref[TARGET_AT + i : TARGET_AT + i + 1, :] for i in range(N)]
    targets[-1] = targets[-1] + table_ref[VOL_AT : VOL_AT + 1, :] * (1.0 / element_total)
    return newton(table_ref, duals, targets, element_total), targets


def middle_kernel(
    element_total,
    gathered_ref, state_ref, up_ref, down_ref, aux_ref,
    new_state_ref, message_ref,
    scaled_ref, stat_ref, table_ref,
):
    duals, targets = update(element_total, gathered_ref, state_ref, table_ref)
    new_state_ref[...] = state_ref[...]
    for i in range(N):
        new_state_ref[i : i + 1, :] = duals[i]
    new_state_ref[TARGET_AT + N - 1 : TARGET_AT + N, :] = targets[-1]
    stat_ref[VOL_AT:, :] = jnp.zeros((LANES - VOL_AT, LANES), jnp.float32)
    evaluate(duals, up_ref, down_ref, aux_ref, scaled_ref, stat_ref)
    announce(stat_ref, message_ref)


def last_kernel(
    element_total,
    gathered_ref, state_ref, up_ref, down_ref, aux_ref, x_ref,
    design_ref, duals_ref,
    table_ref,
):
    duals, _ = update(element_total, gathered_ref, state_ref, table_ref)
    lane = lax.broadcasted_iota(jnp.int32, (1, LANES), 1)
    row = jnp.zeros((1, LANES), jnp.float32)
    for i in range(N):
        row = jnp.where(lane == i, duals[i], row)
    duals_ref[...] = row[:, : duals_ref.shape[1]]
    wide = [jnp.broadcast_to(l, (CHUNK, LANES)) for l in duals]

    def column(j, carry):
        rows = pl.ds(pl.multiple_of(j * CHUNK, CHUNK), CHUNK)
        a, b, lo, hi = (aux_ref[k, rows, :] for k in range(4))
        ups = [up_ref[i, rows, :] for i in range(N)]
        downs = [down_ref[i, rows, :] for i in range(N)]
        _, _, _, t = place(wide, ups, downs, a, b, lo, hi)
        design_ref[rows, :] = x_ref[rows, :] + t
        return carry

    lax.fori_loop(0, aux_ref.shape[1] // CHUNK, column, 0)


def f32(*shape):
    return jax.ShapeDtypeStruct(shape, jnp.float32)


PARAMS = pltpu.CompilerParams(vmem_limit_bytes=16 * 1024 * 1024)
NEAR = ("x", "y")
FAR = ("core", "z")


def per_device(sensitivity, x, x1, x2, gl, gu, w, case_values, duals_start):
    sizes = {name: lax.axis_size(name) for name in ("x", "core", "y", "z")}
    near = sizes["x"] * sizes["y"]
    far = sizes["core"] * sizes["z"]
    cases = sizes["x"] * sizes["core"]
    depth = x.size // LANES
    element_total = float(x.size * near * far)
    shape = x.shape
    x, x1, x2, gl, gu, w = (v.reshape(depth, LANES) for v in (x, x1, x2, gl, gu, w))
    g = lax.all_to_all(
        sensitivity.reshape(cases, depth, LANES), ("x", "core"), split_axis=0, concat_axis=0, tiled=True
    )

    def gather(message):
        heard = lax.all_to_all(message, NEAR, split_axis=0, concat_axis=0, tiled=True)
        part = jnp.broadcast_to(jnp.sum(heard, 0, keepdims=True), (far, LANES))
        return lax.all_to_all(part, FAR, split_axis=0, concat_axis=0, tiled=True)

    lower, upper, aux, volume, state = pl.pallas_call(
        prepare_kernel,
        out_shape=(
            f32(depth, LANES), f32(depth, LANES), f32(4, depth, LANES), f32(8, LANES), f32(STATE, LANES),
        ),
        in_specs=[vmem()] * 8,
        out_specs=(vmem(),) * 5,
        compiler_params=PARAMS,
        cost_estimate=pl.CostEstimate(flops=10_000_000_000, bytes_accessed=40_000_000, transcendentals=0),
    )(duals_start.reshape(1, -1), case_values.reshape(1, -1), x, x1, x2, gl, gu, w)
    work = [pltpu.VMEM((N, depth, LANES), jnp.float32), pltpu.VMEM((LANES, LANES), jnp.float32)]
    table = [pltpu.VMEM((64, LANES), jnp.float32)]
    up, down, message = pl.pallas_call(
        first_kernel,
        out_shape=(f32(N, depth, LANES), f32(N, depth, LANES), f32(near, LANES)),
        in_specs=[vmem()] * 5,
        out_specs=(vmem(),) * 3,
        scratch_shapes=work,
        compiler_params=PARAMS,
    )(g, w, aux, volume, state)
    for _ in range(NEWTON - 1):
        state, message = pl.pallas_call(
            functools.partial(middle_kernel, element_total),
            out_shape=(f32(STATE, LANES), f32(near, LANES)),
            in_specs=[vmem()] * 5,
            out_specs=(vmem(),) * 2,
            scratch_shapes=work + table,
            compiler_params=PARAMS,
        )(gather(message), state, up, down, aux)
    design, duals = pl.pallas_call(
        functools.partial(last_kernel, element_total),
        out_shape=(f32(depth, LANES), f32(1, N)),
        in_specs=[vmem()] * 6,
        out_specs=(vmem(),) * 2,
        scratch_shapes=table,
        compiler_params=PARAMS,
    )(gather(message), state, up, down, aux, x)
    return design.reshape(shape), lower.reshape(shape), upper.reshape(shape), duals.reshape(N)


def solution(mesh):
    cases, slabs = mesh.devices.shape
    fine = Mesh(mesh.devices.reshape(cases // 2, 2, 4, slabs // 4), ("x", "core", "y", "z"))
    case, slab = ("x", "core"), ("y", "z")
    design = P(slab, case, None)
    return jax.shard_map(
        per_device,
        mesh=fine,
        in_specs=(P(case, slab),) + (design,) * 6 + (P(), P()),
        out_specs=(design, design, design, P()),
        check_vma=False,
    )
```

```python
import functools

import jax
import jax.numpy as jnp
from jax import lax
from jax.experimental import pallas as pl
from jax.experimental.pallas import tpu as pltpu
from jax.sharding import Mesh
from jax.sharding import PartitionSpec as P

NEWTON = 4
PROX = 0.1
VOLFRAC = 0.4
N = 9
PAIRS = [(i, k) for i in range(N) for k in range(i + 1)]
GRAD_AT = len(PAIRS)
VOL_AT = GRAD_AT + N
LANES = 128
TARGET_AT = 16
STATE = 32
STATS = 64
CHUNK = 128
KUNROLL = 16
REPEAT_FROM = 2


def vmem():
    return pl.BlockSpec(memory_space=pltpu.VMEM)


def hbm():
    return pl.BlockSpec(memory_space=pltpu.HBM)


def total(rows):
    while rows.shape[0] > 8:
        half = rows.shape[0] // 2
        rows = rows[:half] + rows[half:]
    return jnp.sum(rows, 0, keepdims=True)


def diagonal(values, count):
    row = lax.broadcasted_iota(jnp.int32, (count, LANES), 0)
    lane = lax.broadcasted_iota(jnp.int32, (count, LANES), 1)
    return jnp.where(row == lane, values, 0.0)


def spread(gathered, table_ref):
    sums = jnp.sum(diagonal(total(gathered), table_ref.shape[0]), 1, keepdims=True)
    table_ref[...] = jnp.broadcast_to(sums, table_ref.shape)


def solve(matrix, vector):
    m = dict(matrix)
    b = list(vector)
    inverse = []
    for k in range(N):
        r = 1.0 / m[k, k]
        inverse.append(r)
        for i in range(k + 1, N):
            scaled = m[i, k] * r
            for j in range(k + 1, i + 1):
                m[i, j] = m[i, j] - scaled * m[j, k]
            b[i] = b[i] - scaled * b[k]
    x = [None] * N
    for k in reversed(range(N)):
        running = b[k]
        for i in range(k + 1, N):
            running = running - m[i, k] * x[i]
        x[k] = running * inverse[k]
    return x


def newton(table_ref, duals, targets, element_total):
    scale = 1.0 / element_total
    excess = functools.reduce(jnp.add, duals[:-1]) - 1.0
    height = jnp.maximum(excess, 0.0)
    active = jnp.where(excess > 0, 1.0, 0.0)
    matrix = {}
    for at, (i, k) in enumerate(PAIRS):
        entry = table_ref[at : at + 1, :] * scale
        if i < N - 1:
            entry = entry + active
        matrix[i, k] = entry
    trace = functools.reduce(jnp.add, [matrix[i, i] for i in range(N)])
    damping = trace * (0.5 / N) + 0.0001
    vector = []
    for i in range(N):
        matrix[i, i] = matrix[i, i] + damping
        entry = table_ref[GRAD_AT + i : GRAD_AT + i + 1, :] * scale + targets[i]
        vector.append(entry - height if i < N - 1 else entry)
    step = solve(matrix, vector)
    return [jnp.maximum(l + d, 0.1 * l) for l, d in zip(duals, step)]


def place(duals, slopes, a, b, lo, hi):
    terms = [l * g for l, g in zip(duals, slopes)]
    rise = functools.reduce(jnp.add, [jnp.maximum(m, 0.0) for m in terms])
    fall = functools.reduce(jnp.add, [jnp.minimum(m, 0.0) for m in terms])
    p = PROX + (1.001 * rise - 0.001 * fall)
    q = PROX + (0.001 * rise - 1.001 * fall)
    root_p = p * lax.rsqrt(p)
    root_q = q * lax.rsqrt(q)
    free = a * b * (root_q - root_p) / (a * root_p + b * root_q)
    return p, q, free, jnp.minimum(jnp.maximum(free, lo), hi)


def parts(g_ref, aux_ref):
    return lambda block, k, rows: g_ref[block, k, rows, :] if k < N - 1 else aux_ref[block, k - N + 1, rows, :]


def read(part, block, rows):
    held = [part(block, k, rows) for k in range(N + 4)]
    return held[:N], held[N:]


def evaluate(state_ref, part, scaled_ref, stat_ref, depth, arrive=None):
    blocks = scaled_ref.shape[1] // depth

    def fold(v):
        return jnp.sum(v.reshape(-1, 8, LANES), 0)

    def column(j, grads):
        at = pl.multiple_of(j * CHUNK, CHUNK)
        block = j // (depth // CHUNK)
        rows = pl.ds(pl.multiple_of(at - block * depth, CHUNK), CHUNK)
        if arrive is not None:
            arrive(block)
        slopes, (a, b, lo, hi) = read(part, block, rows)
        duals = [jnp.broadcast_to(state_ref[i : i + 1, :], (CHUNK, LANES)) for i in range(N)]
        p, q, free, t = place(duals, slopes, a, b, lo, hi)
        inside = (free > lo) & (free < hi)
        to_upper = a - t
        to_lower = b + t
        both = 1.0 / (to_upper * to_lower)
        ru = both * to_lower
        rl = both * to_upper
        up_at = a * ru
        down_at = b * rl
        up_two = up_at * up_at
        down_two = down_at * down_at
        curve = 2.0 * (p * up_two * ru + q * down_two * rl)
        root = jnp.where(inside, lax.rsqrt(curve), 0.0)
        cu, cd = up_two * root, down_two * root
        tu, td = t * up_at, t * down_at
        c_rise, c_fall = 1.001 * cu - 0.001 * cd, 1.001 * cd - 0.001 * cu
        t_rise, t_fall = 1.001 * tu - 0.001 * td, 1.001 * td - 0.001 * tu
        out = []
        for i, g in enumerate(slopes):
            rising = g > 0
            scaled_ref[i, pl.ds(at, CHUNK), :] = g * jnp.where(rising, c_rise, c_fall)
            out.append(grads[i] + fold(g * jnp.where(rising, t_rise, t_fall)))
        return tuple(out)

    zero = jnp.zeros((8, LANES), jnp.float32)
    steps = blocks * depth // CHUNK
    grads = lax.fori_loop(0, steps, column, (zero,) * N) if steps > 1 else column(0, (zero,) * N)
    for i in range(N):
        stat_ref[GRAD_AT + i : GRAD_AT + i + 1, :] = jnp.sum(grads[i], 0, keepdims=True)
    groups = [(0, 5), (5, 9)]
    for at, (i0, i1) in enumerate(groups):
        for k0, k1 in groups[: at + 1]:
            pairs = [(i, k) for i in range(i0, i1) for k in range(k0, min(k1, i + 1))]

            def products(j, sums, pairs=pairs):
                rows = pl.ds(pl.multiple_of(j * 8, 8), 8)
                held = {i: scaled_ref[i, rows, :] for i in sorted({i for pair in pairs for i in pair})}
                return tuple(s + held[i] * held[k] for s, (i, k) in zip(sums, pairs))

            sums = lax.fori_loop(0, blocks * depth // 8, products, (zero,) * len(pairs), unroll=KUNROLL)
            for s, pair in zip(sums, pairs):
                row = PAIRS.index(pair)
                stat_ref[row : row + 1, :] = jnp.sum(s, 0, keepdims=True)


def announce(stat_ref, message_ref):
    sums = jnp.sum(stat_ref[...], 1, keepdims=True)
    sums = total(diagonal(sums, stat_ref.shape[0]))
    message_ref[...] = jnp.broadcast_to(sums, message_ref.shape)


def prepare_kernel(
    duals_ref, case_values_ref, x_ref, x1_ref, x2_ref, gl_ref, gu_ref, w_ref,
    lower_ref, upper_ref, aux_ref, volume_ref, state_ref,
):
    x, x1, x2, w = (r[...] for r in (x_ref, x1_ref, x2_ref, w_ref))
    trend = (x - x1) * (x1 - x2)
    factor = jnp.where(trend > 0, 1.2, jnp.where(trend < 0, 0.7, 1.0))
    lower = jnp.minimum(x - factor * gl_ref[...], x - 0.01)
    upper = jnp.maximum(x + factor * gu_ref[...], x + 0.01)
    lower_ref[...] = lower
    upper_ref[...] = upper
    a = upper - x
    b = x - lower
    aux_ref[0, 0] = w
    aux_ref[0, 1] = a
    aux_ref[0, 2] = b
    aux_ref[0, 3] = jnp.maximum(jnp.maximum(lower + 0.1 * b, x - 0.2), 0.0) - x
    aux_ref[0, 4] = jnp.minimum(jnp.minimum(upper - 0.1 * a, x + 0.2), 1.0) - x
    volume_ref[...] = jnp.sum((w * x).reshape(-1, 8, LANES), 0)
    state_ref[...] = jnp.zeros(state_ref.shape, jnp.float32)
    for i in range(N):
        state_ref[i : i + 1, :] = jnp.broadcast_to(duals_ref[0:1, i : i + 1], (1, LANES))
    for i in range(N - 1):
        state_ref[TARGET_AT + i : TARGET_AT + i + 1, :] = jnp.broadcast_to(
            case_values_ref[0:1, i : i + 1], (1, LANES)
        )
    state_ref[TARGET_AT + N - 1 : TARGET_AT + N, :] = jnp.full((1, LANES), -VOLFRAC)


def first_kernel(
    g_ref, aux_ref, volume_ref, state_ref,
    message_ref, pack_ref,
    scaled_ref, stat_ref, sems,
):
    copies = [
        pltpu.make_async_copy(g_ref, pack_ref.at[:, pl.ds(0, N - 1)], sems.at[0]),
        pltpu.make_async_copy(aux_ref, pack_ref.at[:, pl.ds(N - 1, 5)], sems.at[1]),
    ]
    for copy in copies:
        copy.start()
    stat_ref[VOL_AT:, :] = jnp.zeros((STATS - VOL_AT, LANES), jnp.float32)
    stat_ref[VOL_AT : VOL_AT + 1, :] = jnp.sum(volume_ref[...], 0, keepdims=True)
    evaluate(state_ref, parts(g_ref, aux_ref), scaled_ref, stat_ref, aux_ref.shape[2])
    announce(stat_ref, message_ref)
    for copy in copies:
        copy.wait()


def update(element_total, gathered_ref, state_ref, table_ref):
    spread(gathered_ref[...], table_ref)
    duals = [state_ref[i : i + 1, :] for i in range(N)]
    targets = [state_ref[TARGET_AT + i : TARGET_AT + i + 1, :] for i in range(N)]
    targets[-1] = targets[-1] + table_ref[VOL_AT : VOL_AT + 1, :] * (1.0 / element_total)
    return newton(table_ref, duals, targets, element_total), targets


def advance(element_total, gathered_ref, state_ref, new_state_ref, stat_ref, table_ref):
    duals, targets = update(element_total, gathered_ref, state_ref, table_ref)
    new_state_ref[...] = state_ref[...]
    for i in range(N):
        new_state_ref[i : i + 1, :] = duals[i]
    new_state_ref[TARGET_AT + N - 1 : TARGET_AT + N, :] = targets[-1]
    stat_ref[VOL_AT:, :] = jnp.zeros((STATS - VOL_AT, LANES), jnp.float32)


def middle_kernel(
    element_total,
    gathered_ref, state_ref, g_ref, aux_ref,
    new_state_ref, message_ref,
    scaled_ref, stat_ref, table_ref,
):
    advance(element_total, gathered_ref, state_ref, new_state_ref, stat_ref, table_ref)
    evaluate(new_state_ref, parts(g_ref, aux_ref), scaled_ref, stat_ref, aux_ref.shape[2])
    announce(stat_ref, message_ref)


def repeated_kernel(
    element_total,
    gathered_ref, state_ref, pack_ref,
    new_state_ref, message_ref,
    scaled_ref, stat_ref, table_ref, held_ref, sems,
):
    def copy(block):
        return pltpu.make_async_copy(pack_ref.at[block], held_ref.at[block], sems.at[block])

    for block in range(held_ref.shape[0]):
        copy(block).start()
    advance(element_total, gathered_ref, state_ref, new_state_ref, stat_ref, table_ref)

    def part(block, k, rows):
        return held_ref[block, k, rows, :]

    evaluate(new_state_ref, part, scaled_ref, stat_ref, held_ref.shape[2], lambda block: copy(block).wait())
    announce(stat_ref, message_ref)


def last_kernel(
    element_total,
    gathered_ref, state_ref, g_ref, aux_ref, x_ref,
    design_ref, duals_ref,
    table_ref,
):
    duals, _ = update(element_total, gathered_ref, state_ref, table_ref)
    lane = lax.broadcasted_iota(jnp.int32, (1, LANES), 1)
    row = jnp.zeros((1, LANES), jnp.float32)
    for i in range(N):
        row = jnp.where(lane == i, duals[i], row)
    duals_ref[...] = row[:, : duals_ref.shape[1]]
    depth = x_ref.shape[0]
    wide = [jnp.broadcast_to(l, (depth, LANES)) for l in duals]
    slopes, (a, b, lo, hi) = read(parts(g_ref, aux_ref), 0, pl.ds(0, depth))
    _, _, _, t = place(wide, slopes, a, b, lo, hi)
    design_ref[...] = x_ref[...] + t


def f32(*shape):
    return jax.ShapeDtypeStruct(shape, jnp.float32)


PARAMS = pltpu.CompilerParams(vmem_limit_bytes=16 * 1024 * 1024)
WIDE_PARAMS = pltpu.CompilerParams(vmem_limit_bytes=52 * 1024 * 1024)
NEAR = ("x", "y")
FAR = ("core", "z")
REST = ("x", "core", "z")
REPEATED = ("y",)


def scratch(blocks, depth):
    return [
        pltpu.VMEM((N, blocks * depth, LANES), jnp.float32),
        pltpu.VMEM((STATS, LANES), jnp.float32),
        pltpu.VMEM((STATS, LANES), jnp.float32),
    ]


def per_device(sensitivity, x, x1, x2, gl, gu, w, case_values, duals_start):
    sizes = {name: lax.axis_size(name) for name in ("x", "core", "y", "z")}
    near = sizes["x"] * sizes["y"]
    far = sizes["core"] * sizes["z"]
    rest = sizes["x"] * far
    cases = sizes["x"] * sizes["core"]
    depth = x.size // LANES
    element_total = float(x.size * near * far)
    shape = x.shape
    x, x1, x2, gl, gu, w = (v.reshape(depth, LANES) for v in (x, x1, x2, gl, gu, w))
    g = lax.all_to_all(
        sensitivity.reshape(cases, depth, LANES), ("x", "core"), split_axis=0, concat_axis=0, tiled=True
    ).reshape(1, cases, depth, LANES)

    def exchange(message, axes):
        return lax.all_to_all(message, axes, split_axis=0, concat_axis=0, tiled=True)

    def gather(message):
        if message.shape[0] == rest:
            return exchange(message, REST)
        part = jnp.sum(exchange(message, NEAR), 0, keepdims=True)
        return exchange(jnp.broadcast_to(part, (far, LANES)), FAR)

    lower, upper, aux, volume, state = pl.pallas_call(
        prepare_kernel,
        out_shape=(
            f32(depth, LANES), f32(depth, LANES), f32(1, 5, depth, LANES), f32(8, LANES), f32(STATE, LANES),
        ),
        in_specs=[vmem()] * 8,
        out_specs=(vmem(),) * 5,
        compiler_params=PARAMS,
        cost_estimate=pl.CostEstimate(flops=10_000_000_000, bytes_accessed=40_000_000, transcendentals=0),
    )(duals_start.reshape(1, -1), case_values.reshape(1, -1), x, x1, x2, gl, gu, w)
    message, pack = pl.pallas_call(
        first_kernel,
        out_shape=(f32(near, LANES), f32(1, N + 4, depth, LANES)),
        in_specs=[vmem()] * 4,
        out_specs=(vmem(), hbm()),
        scratch_shapes=scratch(1, depth)[:2] + [pltpu.SemaphoreType.DMA((2,))],
        compiler_params=PARAMS,
    )(g, aux, volume, state)
    pack = lax.all_gather(pack, REPEATED, tiled=True)
    blocks = pack.shape[0]
    for step in range(1, NEWTON):
        if step < REPEAT_FROM:
            state, message = pl.pallas_call(
                functools.partial(middle_kernel, element_total),
                out_shape=(f32(STATE, LANES), f32(near, LANES)),
                in_specs=[vmem()] * 4,
                out_specs=(vmem(),) * 2,
                scratch_shapes=scratch(1, depth),
                compiler_params=PARAMS,
            )(gather(message), state, g, aux)
        else:
            state, message = pl.pallas_call(
                functools.partial(repeated_kernel, element_total),
                out_shape=(f32(STATE, LANES), f32(rest, LANES)),
                in_specs=[vmem()] * 2 + [hbm()],
                out_specs=(vmem(),) * 2,
                scratch_shapes=scratch(blocks, depth)
                + [pltpu.VMEM(pack.shape, jnp.float32), pltpu.SemaphoreType.DMA((blocks,))],
                compiler_params=WIDE_PARAMS,
            )(gather(message), state, pack)
    design, duals = pl.pallas_call(
        functools.partial(last_kernel, element_total),
        out_shape=(f32(depth, LANES), f32(1, N)),
        in_specs=[vmem()] * 5,
        out_specs=(vmem(),) * 2,
        scratch_shapes=scratch(1, depth)[2:],
        compiler_params=PARAMS,
    )(gather(message), state, g, aux, x)
    return design.reshape(shape), lower.reshape(shape), upper.reshape(shape), duals.reshape(N)


def solution(mesh):
    cases, slabs = mesh.devices.shape
    fine = Mesh(mesh.devices.reshape(cases // 2, 2, 4, slabs // 4), ("x", "core", "y", "z"))
    case, slab = ("x", "core"), ("y", "z")
    design = P(slab, case, None)
    return jax.shard_map(
        per_device,
        mesh=fine,
        in_specs=(P(case, slab),) + (design,) * 6 + (P(), P()),
        out_specs=(design, design, design, P()),
        check_vma=False,
    )
```

```python
import functools

import jax
import jax.numpy as jnp
from jax import lax
from jax.experimental import pallas as pl
from jax.experimental.pallas import tpu as pltpu
from jax.sharding import Mesh
from jax.sharding import PartitionSpec as P

NEWTON = 4
PROX = 0.1
VOLFRAC = 0.4
N = 9
PAIRS = [(i, k) for i in range(N) for k in range(i + 1)]
GRAD_AT = len(PAIRS)
VOL_AT = GRAD_AT + N
LANES = 128
TARGET_AT = 16
STATE = 32
STATS = 64
CHUNK = 128
KUNROLL = 16


def vmem():
    return pl.BlockSpec(memory_space=pltpu.VMEM)


def total(rows):
    while rows.shape[0] > 8:
        half = rows.shape[0] // 2
        rows = rows[:half] + rows[half:]
    return jnp.sum(rows, 0, keepdims=True)


def diagonal(values, count):
    row = lax.broadcasted_iota(jnp.int32, (count, LANES), 0)
    lane = lax.broadcasted_iota(jnp.int32, (count, LANES), 1)
    return jnp.where(row == lane, values, 0.0)


def spread(gathered, table_ref):
    sums = jnp.sum(diagonal(total(gathered), table_ref.shape[0]), 1, keepdims=True)
    table_ref[...] = jnp.broadcast_to(sums, table_ref.shape)


def solve(matrix, vector):
    m = dict(matrix)
    b = list(vector)
    inverse = []
    for k in range(N):
        r = 1.0 / m[k, k]
        inverse.append(r)
        for i in range(k + 1, N):
            scaled = m[i, k] * r
            for j in range(k + 1, i + 1):
                m[i, j] = m[i, j] - scaled * m[j, k]
            b[i] = b[i] - scaled * b[k]
    x = [None] * N
    for k in reversed(range(N)):
        running = b[k]
        for i in range(k + 1, N):
            running = running - m[i, k] * x[i]
        x[k] = running * inverse[k]
    return x


def newton(table_ref, duals, targets, element_total):
    scale = 1.0 / element_total
    excess = functools.reduce(jnp.add, duals[:-1]) - 1.0
    height = jnp.maximum(excess, 0.0)
    active = jnp.where(excess > 0, 1.0, 0.0)
    matrix = {}
    for at, (i, k) in enumerate(PAIRS):
        entry = table_ref[at : at + 1, :] * scale
        if i < N - 1:
            entry = entry + active
        matrix[i, k] = entry
    trace = functools.reduce(jnp.add, [matrix[i, i] for i in range(N)])
    damping = trace * (0.5 / N) + 0.0001
    vector = []
    for i in range(N):
        matrix[i, i] = matrix[i, i] + damping
        entry = table_ref[GRAD_AT + i : GRAD_AT + i + 1, :] * scale + targets[i]
        vector.append(entry - height if i < N - 1 else entry)
    step = solve(matrix, vector)
    return [jnp.maximum(l + d, 0.1 * l) for l, d in zip(duals, step)]


def place(duals, slopes, a, b, lo, hi):
    terms = [l * g for l, g in zip(duals, slopes)]
    rise = functools.reduce(jnp.add, [jnp.maximum(m, 0.0) for m in terms])
    fall = functools.reduce(jnp.add, [jnp.minimum(m, 0.0) for m in terms])
    p = PROX + (1.001 * rise - 0.001 * fall)
    q = PROX + (0.001 * rise - 1.001 * fall)
    root_p = p * lax.rsqrt(p)
    root_q = q * lax.rsqrt(q)
    free = a * b * (root_q - root_p) / (a * root_p + b * root_q)
    return p, q, free, jnp.minimum(jnp.maximum(free, lo), hi)


def parts(g_ref, aux_ref):
    return lambda block, k, rows: g_ref[block, k, rows, :] if k < N - 1 else aux_ref[block, k - N + 1, rows, :]


def read(part, block, rows):
    held = [part(block, k, rows) for k in range(N + 4)]
    return held[:N], held[N:]


def evaluate(state_ref, part, scaled_ref, stat_ref, depth):
    blocks = scaled_ref.shape[1] // depth

    def fold(v):
        return jnp.sum(v.reshape(-1, 8, LANES), 0)

    def column(j, grads):
        at = pl.multiple_of(j * CHUNK, CHUNK)
        block = j // (depth // CHUNK)
        rows = pl.ds(pl.multiple_of(at - block * depth, CHUNK), CHUNK)
        slopes, (a, b, lo, hi) = read(part, block, rows)
        duals = [jnp.broadcast_to(state_ref[i : i + 1, :], (CHUNK, LANES)) for i in range(N)]
        p, q, free, t = place(duals, slopes, a, b, lo, hi)
        inside = (free > lo) & (free < hi)
        to_upper = a - t
        to_lower = b + t
        both = 1.0 / (to_upper * to_lower)
        ru = both * to_lower
        rl = both * to_upper
        up_at = a * ru
        down_at = b * rl
        up_two = up_at * up_at
        down_two = down_at * down_at
        curve = 2.0 * (p * up_two * ru + q * down_two * rl)
        root = jnp.where(inside, lax.rsqrt(curve), 0.0)
        cu, cd = up_two * root, down_two * root
        tu, td = t * up_at, t * down_at
        c_rise, c_fall = 1.001 * cu - 0.001 * cd, 1.001 * cd - 0.001 * cu
        t_rise, t_fall = 1.001 * tu - 0.001 * td, 1.001 * td - 0.001 * tu
        out = []
        for i, g in enumerate(slopes):
            rising = g > 0
            scaled_ref[i, pl.ds(at, CHUNK), :] = g * jnp.where(rising, c_rise, c_fall)
            out.append(grads[i] + fold(g * jnp.where(rising, t_rise, t_fall)))
        return tuple(out)

    zero = jnp.zeros((8, LANES), jnp.float32)
    steps = blocks * depth // CHUNK
    grads = lax.fori_loop(0, steps, column, (zero,) * N) if steps > 1 else column(0, (zero,) * N)
    for i in range(N):
        stat_ref[GRAD_AT + i : GRAD_AT + i + 1, :] = jnp.sum(grads[i], 0, keepdims=True)
    groups = [(0, 5), (5, 9)]
    for at, (i0, i1) in enumerate(groups):
        for k0, k1 in groups[: at + 1]:
            pairs = [(i, k) for i in range(i0, i1) for k in range(k0, min(k1, i + 1))]

            def products(j, sums, pairs=pairs):
                rows = pl.ds(pl.multiple_of(j * 8, 8), 8)
                held = {i: scaled_ref[i, rows, :] for i in sorted({i for pair in pairs for i in pair})}
                return tuple(s + held[i] * held[k] for s, (i, k) in zip(sums, pairs))

            sums = lax.fori_loop(0, blocks * depth // 8, products, (zero,) * len(pairs), unroll=KUNROLL)
            for s, pair in zip(sums, pairs):
                row = PAIRS.index(pair)
                stat_ref[row : row + 1, :] = jnp.sum(s, 0, keepdims=True)


def announce(stat_ref, message_ref):
    sums = jnp.sum(stat_ref[...], 1, keepdims=True)
    sums = total(diagonal(sums, stat_ref.shape[0]))
    message_ref[...] = jnp.broadcast_to(sums, message_ref.shape)


def prepare_kernel(
    duals_ref, case_values_ref, x_ref, x1_ref, x2_ref, gl_ref, gu_ref, w_ref,
    lower_ref, upper_ref, aux_ref, volume_ref, state_ref,
):
    x, x1, x2, w = (r[...] for r in (x_ref, x1_ref, x2_ref, w_ref))
    trend = (x - x1) * (x1 - x2)
    factor = jnp.where(trend > 0, 1.2, jnp.where(trend < 0, 0.7, 1.0))
    lower = jnp.minimum(x - factor * gl_ref[...], x - 0.01)
    upper = jnp.maximum(x + factor * gu_ref[...], x + 0.01)
    lower_ref[...] = lower
    upper_ref[...] = upper
    a = upper - x
    b = x - lower
    aux_ref[0, 0] = w
    aux_ref[0, 1] = a
    aux_ref[0, 2] = b
    aux_ref[0, 3] = jnp.maximum(jnp.maximum(lower + 0.1 * b, x - 0.2), 0.0) - x
    aux_ref[0, 4] = jnp.minimum(jnp.minimum(upper - 0.1 * a, x + 0.2), 1.0) - x
    volume_ref[...] = jnp.sum((w * x).reshape(-1, 8, LANES), 0)
    state_ref[...] = jnp.zeros(state_ref.shape, jnp.float32)
    for i in range(N):
        state_ref[i : i + 1, :] = jnp.broadcast_to(duals_ref[0:1, i : i + 1], (1, LANES))
    for i in range(N - 1):
        state_ref[TARGET_AT + i : TARGET_AT + i + 1, :] = jnp.broadcast_to(
            case_values_ref[0:1, i : i + 1], (1, LANES)
        )
    state_ref[TARGET_AT + N - 1 : TARGET_AT + N, :] = jnp.full((1, LANES), -VOLFRAC)


def first_kernel(g_ref, aux_ref, volume_ref, state_ref, message_ref, scaled_ref, stat_ref):
    stat_ref[VOL_AT:, :] = jnp.zeros((STATS - VOL_AT, LANES), jnp.float32)
    stat_ref[VOL_AT : VOL_AT + 1, :] = jnp.sum(volume_ref[...], 0, keepdims=True)
    evaluate(state_ref, parts(g_ref, aux_ref), scaled_ref, stat_ref, aux_ref.shape[2])
    announce(stat_ref, message_ref)


def update(element_total, gathered_ref, state_ref, table_ref):
    spread(gathered_ref[...], table_ref)
    duals = [state_ref[i : i + 1, :] for i in range(N)]
    targets = [state_ref[TARGET_AT + i : TARGET_AT + i + 1, :] for i in range(N)]
    targets[-1] = targets[-1] + table_ref[VOL_AT : VOL_AT + 1, :] * (1.0 / element_total)
    return newton(table_ref, duals, targets, element_total), targets


def advance(element_total, gathered_ref, state_ref, new_state_ref, stat_ref, table_ref):
    duals, targets = update(element_total, gathered_ref, state_ref, table_ref)
    new_state_ref[...] = state_ref[...]
    for i in range(N):
        new_state_ref[i : i + 1, :] = duals[i]
    new_state_ref[TARGET_AT + N - 1 : TARGET_AT + N, :] = targets[-1]
    stat_ref[VOL_AT:, :] = jnp.zeros((STATS - VOL_AT, LANES), jnp.float32)


def middle_kernel(
    element_total,
    gathered_ref, state_ref, g_ref, aux_ref,
    new_state_ref, message_ref,
    scaled_ref, stat_ref, table_ref,
):
    advance(element_total, gathered_ref, state_ref, new_state_ref, stat_ref, table_ref)
    evaluate(new_state_ref, parts(g_ref, aux_ref), scaled_ref, stat_ref, aux_ref.shape[2])
    announce(stat_ref, message_ref)


def last_kernel(
    element_total,
    gathered_ref, state_ref, g_ref, aux_ref, x_ref,
    design_ref, duals_ref,
    table_ref,
):
    duals, _ = update(element_total, gathered_ref, state_ref, table_ref)
    lane = lax.broadcasted_iota(jnp.int32, (1, LANES), 1)
    row = jnp.zeros((1, LANES), jnp.float32)
    for i in range(N):
        row = jnp.where(lane == i, duals[i], row)
    duals_ref[...] = row[:, : duals_ref.shape[1]]
    depth = x_ref.shape[0]
    wide = [jnp.broadcast_to(l, (depth, LANES)) for l in duals]
    slopes, (a, b, lo, hi) = read(parts(g_ref, aux_ref), 0, pl.ds(0, depth))
    _, _, _, t = place(wide, slopes, a, b, lo, hi)
    design_ref[...] = x_ref[...] + t


def f32(*shape):
    return jax.ShapeDtypeStruct(shape, jnp.float32)


PARAMS = pltpu.CompilerParams(vmem_limit_bytes=16 * 1024 * 1024)
NEAR = ("x", "y")
FAR = ("core", "z")


def scratch(blocks, depth):
    return [
        pltpu.VMEM((N, blocks * depth, LANES), jnp.float32),
        pltpu.VMEM((STATS, LANES), jnp.float32),
        pltpu.VMEM((STATS, LANES), jnp.float32),
    ]


def per_device(sensitivity, x, x1, x2, gl, gu, w, case_values, duals_start):
    sizes = {name: lax.axis_size(name) for name in ("x", "core", "y", "z")}
    near = sizes["x"] * sizes["y"]
    far = sizes["core"] * sizes["z"]
    cases = sizes["x"] * sizes["core"]
    depth = x.size // LANES
    element_total = float(x.size * near * far)
    shape = x.shape
    x, x1, x2, gl, gu, w = (v.reshape(depth, LANES) for v in (x, x1, x2, gl, gu, w))
    g = lax.all_to_all(
        sensitivity.reshape(cases, depth, LANES), ("x", "core"), split_axis=0, concat_axis=0, tiled=True
    ).reshape(1, cases, depth, LANES)

    def exchange(message, axes):
        return lax.all_to_all(message, axes, split_axis=0, concat_axis=0, tiled=True)

    def gather(message):
        part = jnp.sum(exchange(message, NEAR), 0, keepdims=True)
        return exchange(jnp.broadcast_to(part, (far, LANES)), FAR)

    lower, upper, aux, volume, state = pl.pallas_call(
        prepare_kernel,
        out_shape=(
            f32(depth, LANES), f32(depth, LANES), f32(1, 5, depth, LANES), f32(8, LANES), f32(STATE, LANES),
        ),
        in_specs=[vmem()] * 8,
        out_specs=(vmem(),) * 5,
        compiler_params=PARAMS,
        cost_estimate=pl.CostEstimate(flops=10_000_000_000, bytes_accessed=40_000_000, transcendentals=0),
    )(duals_start.reshape(1, -1), case_values.reshape(1, -1), x, x1, x2, gl, gu, w)
    message = pl.pallas_call(
        first_kernel,
        out_shape=f32(near, LANES),
        in_specs=[vmem()] * 4,
        out_specs=vmem(),
        scratch_shapes=scratch(1, depth)[:2],
        compiler_params=PARAMS,
    )(g, aux, volume, state)
    for _ in range(NEWTON - 1):
        state, message = pl.pallas_call(
            functools.partial(middle_kernel, element_total),
            out_shape=(f32(STATE, LANES), f32(near, LANES)),
            in_specs=[vmem()] * 4,
            out_specs=(vmem(),) * 2,
            scratch_shapes=scratch(1, depth),
            compiler_params=PARAMS,
        )(gather(message), state, g, aux)
    design, duals = pl.pallas_call(
        functools.partial(last_kernel, element_total),
        out_shape=(f32(depth, LANES), f32(1, N)),
        in_specs=[vmem()] * 5,
        out_specs=(vmem(),) * 2,
        scratch_shapes=scratch(1, depth)[2:],
        compiler_params=PARAMS,
    )(gather(message), state, g, aux, x)
    return design.reshape(shape), lower.reshape(shape), upper.reshape(shape), duals.reshape(N)


def solution(mesh):
    cases, slabs = mesh.devices.shape
    fine = Mesh(mesh.devices.reshape(cases // 2, 2, 4, slabs // 4), ("x", "core", "y", "z"))
    case, slab = ("x", "core"), ("y", "z")
    design = P(slab, case, None)
    return jax.shard_map(
        per_device,
        mesh=fine,
        in_specs=(P(case, slab),) + (design,) * 6 + (P(), P()),
        out_specs=(design, design, design, P()),
        check_vma=False,
    )
```

```python
import functools

import jax
import jax.numpy as jnp
from jax import lax
from jax.experimental import pallas as pl
from jax.experimental.pallas import tpu as pltpu
from jax.sharding import Mesh
from jax.sharding import PartitionSpec as P

NEWTON = 4
PROX = 0.1
VOLFRAC = 0.4
N = 9
PAIRS = [(i, k) for i in range(N) for k in range(i + 1)]
GRAD_AT = len(PAIRS)
VOL_AT = GRAD_AT + N
LANES = 128
TARGET_AT = 16
STATE = 32
STATS = 64
CHUNK = 128
KUNROLL = 16
ORDER = ("nf", "nf", "nf", "fn")


def vmem():
    return pl.BlockSpec(memory_space=pltpu.VMEM)


def total(rows):
    while rows.shape[0] > 8:
        half = rows.shape[0] // 2
        rows = rows[:half] + rows[half:]
    return jnp.sum(rows, 0, keepdims=True)


def diagonal(values, count):
    row = lax.broadcasted_iota(jnp.int32, (count, LANES), 0)
    lane = lax.broadcasted_iota(jnp.int32, (count, LANES), 1)
    return jnp.where(row == lane, values, 0.0)


def spread(gathered, table_ref):
    sums = jnp.sum(diagonal(total(gathered), table_ref.shape[0]), 1, keepdims=True)
    table_ref[...] = jnp.broadcast_to(sums, table_ref.shape)


def solve(matrix, vector):
    m = dict(matrix)
    b = list(vector)
    inverse = []
    for k in range(N):
        r = 1.0 / m[k, k]
        inverse.append(r)
        for i in range(k + 1, N):
            scaled = m[i, k] * r
            for j in range(k + 1, i + 1):
                m[i, j] = m[i, j] - scaled * m[j, k]
            b[i] = b[i] - scaled * b[k]
    x = [None] * N
    for k in reversed(range(N)):
        running = b[k]
        for i in range(k + 1, N):
            running = running - m[i, k] * x[i]
        x[k] = running * inverse[k]
    return x


def newton(table_ref, duals, targets, element_total):
    scale = 1.0 / element_total
    excess = functools.reduce(jnp.add, duals[:-1]) - 1.0
    height = jnp.maximum(excess, 0.0)
    active = jnp.where(excess > 0, 1.0, 0.0)
    matrix = {}
    for at, (i, k) in enumerate(PAIRS):
        entry = table_ref[at : at + 1, :] * scale
        if i < N - 1:
            entry = entry + active
        matrix[i, k] = entry
    trace = functools.reduce(jnp.add, [matrix[i, i] for i in range(N)])
    damping = trace * (0.5 / N) + 0.0001
    vector = []
    for i in range(N):
        matrix[i, i] = matrix[i, i] + damping
        entry = table_ref[GRAD_AT + i : GRAD_AT + i + 1, :] * scale + targets[i]
        vector.append(entry - height if i < N - 1 else entry)
    step = solve(matrix, vector)
    return [jnp.maximum(l + d, 0.1 * l) for l, d in zip(duals, step)]


def place(duals, slopes, a, b, lo, hi):
    terms = [l * g for l, g in zip(duals, slopes)]
    rise = functools.reduce(jnp.add, [jnp.maximum(m, 0.0) for m in terms])
    fall = functools.reduce(jnp.add, [jnp.minimum(m, 0.0) for m in terms])
    p = PROX + (1.001 * rise - 0.001 * fall)
    q = PROX + (0.001 * rise - 1.001 * fall)
    root_p = p * lax.rsqrt(p)
    root_q = q * lax.rsqrt(q)
    free = a * b * (root_q - root_p) / (a * root_p + b * root_q)
    return p, q, free, jnp.minimum(jnp.maximum(free, lo), hi)


def parts(g_ref, aux_ref):
    return lambda block, k, rows: g_ref[block, k, rows, :] if k < N - 1 else aux_ref[block, k - N + 1, rows, :]


def read(part, block, rows):
    held = [part(block, k, rows) for k in range(N + 4)]
    return held[:N], held[N:]


def evaluate(state_ref, part, scaled_ref, stat_ref, depth):
    blocks = scaled_ref.shape[1] // depth

    def fold(v):
        return jnp.sum(v.reshape(-1, 8, LANES), 0)

    def column(j, grads):
        at = pl.multiple_of(j * CHUNK, CHUNK)
        block = j // (depth // CHUNK)
        rows = pl.ds(pl.multiple_of(at - block * depth, CHUNK), CHUNK)
        slopes, (a, b, lo, hi) = read(part, block, rows)
        duals = [jnp.broadcast_to(state_ref[i : i + 1, :], (CHUNK, LANES)) for i in range(N)]
        p, q, free, t = place(duals, slopes, a, b, lo, hi)
        inside = (free > lo) & (free < hi)
        to_upper = a - t
        to_lower = b + t
        both = 1.0 / (to_upper * to_lower)
        ru = both * to_lower
        rl = both * to_upper
        up_at = a * ru
        down_at = b * rl
        up_two = up_at * up_at
        down_two = down_at * down_at
        curve = 2.0 * (p * up_two * ru + q * down_two * rl)
        root = jnp.where(inside, lax.rsqrt(curve), 0.0)
        cu, cd = up_two * root, down_two * root
        tu, td = t * up_at, t * down_at
        c_rise, c_fall = 1.001 * cu - 0.001 * cd, 1.001 * cd - 0.001 * cu
        t_rise, t_fall = 1.001 * tu - 0.001 * td, 1.001 * td - 0.001 * tu
        out = []
        for i, g in enumerate(slopes):
            rising = g > 0
            scaled_ref[i, pl.ds(at, CHUNK), :] = g * jnp.where(rising, c_rise, c_fall)
            out.append(grads[i] + fold(g * jnp.where(rising, t_rise, t_fall)))
        return tuple(out)

    zero = jnp.zeros((8, LANES), jnp.float32)
    steps = blocks * depth // CHUNK
    grads = lax.fori_loop(0, steps, column, (zero,) * N) if steps > 1 else column(0, (zero,) * N)
    for i in range(N):
        stat_ref[GRAD_AT + i : GRAD_AT + i + 1, :] = jnp.sum(grads[i], 0, keepdims=True)
    groups = [(0, 5), (5, 9)]
    for at, (i0, i1) in enumerate(groups):
        for k0, k1 in groups[: at + 1]:
            pairs = [(i, k) for i in range(i0, i1) for k in range(k0, min(k1, i + 1))]

            def products(j, sums, pairs=pairs):
                rows = pl.ds(pl.multiple_of(j * 8, 8), 8)
                held = {i: scaled_ref[i, rows, :] for i in sorted({i for pair in pairs for i in pair})}
                return tuple(s + held[i] * held[k] for s, (i, k) in zip(sums, pairs))

            sums = lax.fori_loop(0, blocks * depth // 8, products, (zero,) * len(pairs), unroll=KUNROLL)
            for s, pair in zip(sums, pairs):
                row = PAIRS.index(pair)
                stat_ref[row : row + 1, :] = jnp.sum(s, 0, keepdims=True)


def announce(stat_ref, message_ref):
    sums = jnp.sum(stat_ref[...], 1, keepdims=True)
    sums = total(diagonal(sums, stat_ref.shape[0]))
    message_ref[...] = jnp.broadcast_to(sums, message_ref.shape)


def prepare_kernel(
    duals_ref, case_values_ref, x_ref, x1_ref, x2_ref, gl_ref, gu_ref, w_ref,
    lower_ref, upper_ref, aux_ref, volume_ref, state_ref,
):
    x, x1, x2, w = (r[...] for r in (x_ref, x1_ref, x2_ref, w_ref))
    trend = (x - x1) * (x1 - x2)
    factor = jnp.where(trend > 0, 1.2, jnp.where(trend < 0, 0.7, 1.0))
    lower = jnp.minimum(x - factor * gl_ref[...], x - 0.01)
    upper = jnp.maximum(x + factor * gu_ref[...], x + 0.01)
    lower_ref[...] = lower
    upper_ref[...] = upper
    a = upper - x
    b = x - lower
    aux_ref[0, 0] = w
    aux_ref[0, 1] = a
    aux_ref[0, 2] = b
    aux_ref[0, 3] = jnp.maximum(jnp.maximum(lower + 0.1 * b, x - 0.2), 0.0) - x
    aux_ref[0, 4] = jnp.minimum(jnp.minimum(upper - 0.1 * a, x + 0.2), 1.0) - x
    volume_ref[...] = jnp.sum((w * x).reshape(-1, 8, LANES), 0)
    state_ref[...] = jnp.zeros(state_ref.shape, jnp.float32)
    for i in range(N):
        state_ref[i : i + 1, :] = jnp.broadcast_to(duals_ref[0:1, i : i + 1], (1, LANES))
    for i in range(N - 1):
        state_ref[TARGET_AT + i : TARGET_AT + i + 1, :] = jnp.broadcast_to(
            case_values_ref[0:1, i : i + 1], (1, LANES)
        )
    state_ref[TARGET_AT + N - 1 : TARGET_AT + N, :] = jnp.full((1, LANES), -VOLFRAC)


def first_kernel(g_ref, aux_ref, volume_ref, state_ref, message_ref, scaled_ref, stat_ref):
    stat_ref[VOL_AT:, :] = jnp.zeros((STATS - VOL_AT, LANES), jnp.float32)
    stat_ref[VOL_AT : VOL_AT + 1, :] = jnp.sum(volume_ref[...], 0, keepdims=True)
    evaluate(state_ref, parts(g_ref, aux_ref), scaled_ref, stat_ref, aux_ref.shape[2])
    announce(stat_ref, message_ref)


def update(element_total, gathered_ref, state_ref, table_ref):
    spread(gathered_ref[...], table_ref)
    duals = [state_ref[i : i + 1, :] for i in range(N)]
    targets = [state_ref[TARGET_AT + i : TARGET_AT + i + 1, :] for i in range(N)]
    targets[-1] = targets[-1] + table_ref[VOL_AT : VOL_AT + 1, :] * (1.0 / element_total)
    return newton(table_ref, duals, targets, element_total), targets


def advance(element_total, gathered_ref, state_ref, new_state_ref, stat_ref, table_ref):
    duals, targets = update(element_total, gathered_ref, state_ref, table_ref)
    new_state_ref[...] = state_ref[...]
    for i in range(N):
        new_state_ref[i : i + 1, :] = duals[i]
    new_state_ref[TARGET_AT + N - 1 : TARGET_AT + N, :] = targets[-1]
    stat_ref[VOL_AT:, :] = jnp.zeros((STATS - VOL_AT, LANES), jnp.float32)


def middle_kernel(
    element_total,
    gathered_ref, state_ref, g_ref, aux_ref,
    new_state_ref, message_ref,
    scaled_ref, stat_ref, table_ref,
):
    advance(element_total, gathered_ref, state_ref, new_state_ref, stat_ref, table_ref)
    evaluate(new_state_ref, parts(g_ref, aux_ref), scaled_ref, stat_ref, aux_ref.shape[2])
    announce(stat_ref, message_ref)


def last_kernel(
    element_total,
    gathered_ref, state_ref, g_ref, aux_ref, x_ref,
    design_ref, duals_ref,
    table_ref,
):
    duals, _ = update(element_total, gathered_ref, state_ref, table_ref)
    lane = lax.broadcasted_iota(jnp.int32, (1, LANES), 1)
    row = jnp.zeros((1, LANES), jnp.float32)
    for i in range(N):
        row = jnp.where(lane == i, duals[i], row)
    duals_ref[...] = row[:, : duals_ref.shape[1]]
    depth = x_ref.shape[0]
    wide = [jnp.broadcast_to(l, (depth, LANES)) for l in duals]
    slopes, (a, b, lo, hi) = read(parts(g_ref, aux_ref), 0, pl.ds(0, depth))
    _, _, _, t = place(wide, slopes, a, b, lo, hi)
    design_ref[...] = x_ref[...] + t


def f32(*shape):
    return jax.ShapeDtypeStruct(shape, jnp.float32)


PARAMS = pltpu.CompilerParams(vmem_limit_bytes=16 * 1024 * 1024)
NEAR = ("x", "y")
FAR = ("core", "z")


def scratch(blocks, depth):
    return [
        pltpu.VMEM((N, blocks * depth, LANES), jnp.float32),
        pltpu.VMEM((STATS, LANES), jnp.float32),
        pltpu.VMEM((STATS, LANES), jnp.float32),
    ]


def per_device(sensitivity, x, x1, x2, gl, gu, w, case_values, duals_start):
    sizes = {name: lax.axis_size(name) for name in ("x", "core", "y", "z")}
    near = sizes["x"] * sizes["y"]
    far = sizes["core"] * sizes["z"]
    cases = sizes["x"] * sizes["core"]
    depth = x.size // LANES
    element_total = float(x.size * near * far)
    shape = x.shape
    x, x1, x2, gl, gu, w = (v.reshape(depth, LANES) for v in (x, x1, x2, gl, gu, w))
    g = lax.all_to_all(
        sensitivity.reshape(cases, depth, LANES), ("x", "core"), split_axis=0, concat_axis=0, tiled=True
    ).reshape(1, cases, depth, LANES)

    def exchange(message, axes):
        return lax.all_to_all(message, axes, split_axis=0, concat_axis=0, tiled=True)

    stages = {"n": (NEAR, near), "f": (FAR, far)}

    def gather(message, order):
        (first, _), (second, count) = (stages[name] for name in order)
        part = jnp.sum(exchange(message, first), 0, keepdims=True)
        return exchange(jnp.broadcast_to(part, (count, LANES)), second)

    lower, upper, aux, volume, state = pl.pallas_call(
        prepare_kernel,
        out_shape=(
            f32(depth, LANES), f32(depth, LANES), f32(1, 5, depth, LANES), f32(8, LANES), f32(STATE, LANES),
        ),
        in_specs=[vmem()] * 8,
        out_specs=(vmem(),) * 5,
        compiler_params=PARAMS,
        cost_estimate=pl.CostEstimate(flops=10_000_000_000, bytes_accessed=40_000_000, transcendentals=0),
    )(duals_start.reshape(1, -1), case_values.reshape(1, -1), x, x1, x2, gl, gu, w)
    message = pl.pallas_call(
        first_kernel,
        out_shape=f32(stages[ORDER[0][0]][1], LANES),
        in_specs=[vmem()] * 4,
        out_specs=vmem(),
        scratch_shapes=scratch(1, depth)[:2],
        compiler_params=PARAMS,
    )(g, aux, volume, state)
    for step in range(1, NEWTON):
        state, message = pl.pallas_call(
            functools.partial(middle_kernel, element_total),
            out_shape=(f32(STATE, LANES), f32(stages[ORDER[step][0]][1], LANES)),
            in_specs=[vmem()] * 4,
            out_specs=(vmem(),) * 2,
            scratch_shapes=scratch(1, depth),
            compiler_params=PARAMS,
        )(gather(message, ORDER[step - 1]), state, g, aux)
    design, duals = pl.pallas_call(
        functools.partial(last_kernel, element_total),
        out_shape=(f32(depth, LANES), f32(1, N)),
        in_specs=[vmem()] * 5,
        out_specs=(vmem(),) * 2,
        scratch_shapes=scratch(1, depth)[2:],
        compiler_params=PARAMS,
    )(gather(message, ORDER[-1]), state, g, aux, x)
    return design.reshape(shape), lower.reshape(shape), upper.reshape(shape), duals.reshape(N)


def solution(mesh):
    cases, slabs = mesh.devices.shape
    fine = Mesh(mesh.devices.reshape(cases // 2, 2, 4, slabs // 4), ("x", "core", "y", "z"))
    case, slab = ("x", "core"), ("y", "z")
    design = P(slab, case, None)
    return jax.shard_map(
        per_device,
        mesh=fine,
        in_specs=(P(case, slab),) + (design,) * 6 + (P(), P()),
        out_specs=(design, design, design, P()),
        check_vma=False,
    )
```

```python
import functools

import jax
import jax.numpy as jnp
from jax import lax
from jax.experimental import pallas as pl
from jax.experimental.pallas import tpu as pltpu
from jax.sharding import Mesh
from jax.sharding import PartitionSpec as P

NEWTON = 4
PROX = 0.1
VOLFRAC = 0.4
N = 9
PAIRS = [(i, k) for i in range(N) for k in range(i + 1)]
GRAD_AT = len(PAIRS)
VOL_AT = GRAD_AT + N
LANES = 128
TARGET_AT = 16
STATE = 32
STATS = 64
CHUNK = 128
KUNROLL = 16


def vmem():
    return pl.BlockSpec(memory_space=pltpu.VMEM)


def total(rows):
    while rows.shape[0] > 8:
        half = rows.shape[0] // 2
        rows = rows[:half] + rows[half:]
    return jnp.sum(rows, 0, keepdims=True)


def diagonal(values, count):
    row = lax.broadcasted_iota(jnp.int32, (count, LANES), 0)
    lane = lax.broadcasted_iota(jnp.int32, (count, LANES), 1)
    return jnp.where(row == lane, values, 0.0)


def spread(gathered, table_ref):
    sums = jnp.sum(diagonal(total(gathered), table_ref.shape[0]), 1, keepdims=True)
    table_ref[...] = jnp.broadcast_to(sums, table_ref.shape)


def solve(matrix, vector):
    m = dict(matrix)
    b = list(vector)
    inverse = []
    for k in range(N):
        r = 1.0 / m[k, k]
        inverse.append(r)
        for i in range(k + 1, N):
            scaled = m[i, k] * r
            for j in range(k + 1, i + 1):
                m[i, j] = m[i, j] - scaled * m[j, k]
            b[i] = b[i] - scaled * b[k]
    x = [None] * N
    for k in reversed(range(N)):
        running = b[k]
        for i in range(k + 1, N):
            running = running - m[i, k] * x[i]
        x[k] = running * inverse[k]
    return x


def newton(table_ref, duals, targets, element_total):
    scale = 1.0 / element_total
    excess = functools.reduce(jnp.add, duals[:-1]) - 1.0
    height = jnp.maximum(excess, 0.0)
    active = jnp.where(excess > 0, 1.0, 0.0)
    matrix = {}
    for at, (i, k) in enumerate(PAIRS):
        entry = table_ref[at : at + 1, :] * scale
        if i < N - 1:
            entry = entry + active
        matrix[i, k] = entry
    trace = functools.reduce(jnp.add, [matrix[i, i] for i in range(N)])
    damping = trace * (0.5 / N) + 0.0001
    vector = []
    for i in range(N):
        matrix[i, i] = matrix[i, i] + damping
        entry = table_ref[GRAD_AT + i : GRAD_AT + i + 1, :] * scale + targets[i]
        vector.append(entry - height if i < N - 1 else entry)
    step = solve(matrix, vector)
    return [jnp.maximum(l + d, 0.1 * l) for l, d in zip(duals, step)]


def place(duals, slopes, a, b, lo, hi):
    terms = [l * g for l, g in zip(duals, slopes)]
    rise = functools.reduce(jnp.add, [jnp.maximum(m, 0.0) for m in terms])
    fall = functools.reduce(jnp.add, [jnp.minimum(m, 0.0) for m in terms])
    p = PROX + (1.001 * rise - 0.001 * fall)
    q = PROX + (0.001 * rise - 1.001 * fall)
    root_p = p * lax.rsqrt(p)
    root_q = q * lax.rsqrt(q)
    free = a * b * (root_q - root_p) / (a * root_p + b * root_q)
    return p, q, free, jnp.minimum(jnp.maximum(free, lo), hi)


def parts(g_ref, aux_ref):
    return lambda block, k, rows: g_ref[block, k, rows, :] if k < N - 1 else aux_ref[block, k - N + 1, rows, :]


def read(part, block, rows):
    held = [part(block, k, rows) for k in range(N + 4)]
    return held[:N], held[N:]


def evaluate(state_ref, part, scaled_ref, stat_ref, depth):
    blocks = scaled_ref.shape[1] // depth

    def fold(v):
        return jnp.sum(v.reshape(-1, 8, LANES), 0)

    def column(j, grads):
        at = pl.multiple_of(j * CHUNK, CHUNK)
        block = j // (depth // CHUNK)
        rows = pl.ds(pl.multiple_of(at - block * depth, CHUNK), CHUNK)
        slopes, (a, b, lo, hi) = read(part, block, rows)
        duals = [jnp.broadcast_to(state_ref[i : i + 1, :], (CHUNK, LANES)) for i in range(N)]
        p, q, free, t = place(duals, slopes, a, b, lo, hi)
        inside = (free > lo) & (free < hi)
        to_upper = a - t
        to_lower = b + t
        both = 1.0 / (to_upper * to_lower)
        ru = both * to_lower
        rl = both * to_upper
        up_at = a * ru
        down_at = b * rl
        up_two = up_at * up_at
        down_two = down_at * down_at
        curve = 2.0 * (p * up_two * ru + q * down_two * rl)
        root = jnp.where(inside, lax.rsqrt(curve), 0.0)
        cu, cd = up_two * root, down_two * root
        tu, td = t * up_at, t * down_at
        c_rise, c_fall = 1.001 * cu - 0.001 * cd, 1.001 * cd - 0.001 * cu
        t_rise, t_fall = 1.001 * tu - 0.001 * td, 1.001 * td - 0.001 * tu
        out = []
        for i, g in enumerate(slopes):
            rising = g > 0
            scaled_ref[i, pl.ds(at, CHUNK), :] = g * jnp.where(rising, c_rise, c_fall)
            out.append(grads[i] + fold(g * jnp.where(rising, t_rise, t_fall)))
        return tuple(out)

    zero = jnp.zeros((8, LANES), jnp.float32)
    steps = blocks * depth // CHUNK
    grads = lax.fori_loop(0, steps, column, (zero,) * N) if steps > 1 else column(0, (zero,) * N)
    for i in range(N):
        stat_ref[GRAD_AT + i : GRAD_AT + i + 1, :] = jnp.sum(grads[i], 0, keepdims=True)
    groups = [(0, 5), (5, 9)]
    for at, (i0, i1) in enumerate(groups):
        for k0, k1 in groups[: at + 1]:
            pairs = [(i, k) for i in range(i0, i1) for k in range(k0, min(k1, i + 1))]

            def products(j, sums, pairs=pairs):
                rows = pl.ds(pl.multiple_of(j * 8, 8), 8)
                held = {i: scaled_ref[i, rows, :] for i in sorted({i for pair in pairs for i in pair})}
                return tuple(s + held[i] * held[k] for s, (i, k) in zip(sums, pairs))

            sums = lax.fori_loop(0, blocks * depth // 8, products, (zero,) * len(pairs), unroll=KUNROLL)
            for s, pair in zip(sums, pairs):
                row = PAIRS.index(pair)
                stat_ref[row : row + 1, :] = jnp.sum(s, 0, keepdims=True)


def announce(stat_ref, message_ref):
    sums = jnp.sum(stat_ref[...], 1, keepdims=True)
    sums = total(diagonal(sums, stat_ref.shape[0]))
    message_ref[...] = jnp.broadcast_to(sums, message_ref.shape)


def prepare_kernel(
    duals_ref, case_values_ref, x_ref, x1_ref, x2_ref, gl_ref, gu_ref, w_ref,
    lower_ref, upper_ref, aux_ref, volume_ref, state_ref,
):
    x, x1, x2, w = (r[...] for r in (x_ref, x1_ref, x2_ref, w_ref))
    trend = (x - x1) * (x1 - x2)
    factor = jnp.where(trend > 0, 1.2, jnp.where(trend < 0, 0.7, 1.0))
    lower = jnp.minimum(x - factor * gl_ref[...], x - 0.01)
    upper = jnp.maximum(x + factor * gu_ref[...], x + 0.01)
    lower_ref[...] = lower
    upper_ref[...] = upper
    a = upper - x
    b = x - lower
    aux_ref[0, 0] = w
    aux_ref[0, 1] = a
    aux_ref[0, 2] = b
    aux_ref[0, 3] = jnp.maximum(jnp.maximum(lower + 0.1 * b, x - 0.2), 0.0) - x
    aux_ref[0, 4] = jnp.minimum(jnp.minimum(upper - 0.1 * a, x + 0.2), 1.0) - x
    volume_ref[...] = jnp.sum((w * x).reshape(-1, 8, LANES), 0)
    state_ref[...] = jnp.zeros(state_ref.shape, jnp.float32)
    for i in range(N):
        state_ref[i : i + 1, :] = jnp.broadcast_to(duals_ref[0:1, i : i + 1], (1, LANES))
    for i in range(N - 1):
        state_ref[TARGET_AT + i : TARGET_AT + i + 1, :] = jnp.broadcast_to(
            case_values_ref[0:1, i : i + 1], (1, LANES)
        )
    state_ref[TARGET_AT + N - 1 : TARGET_AT + N, :] = jnp.full((1, LANES), -VOLFRAC)


def first_kernel(g_ref, aux_ref, volume_ref, state_ref, message_ref, scaled_ref, stat_ref):
    stat_ref[VOL_AT:, :] = jnp.zeros((STATS - VOL_AT, LANES), jnp.float32)
    stat_ref[VOL_AT : VOL_AT + 1, :] = jnp.sum(volume_ref[...], 0, keepdims=True)
    evaluate(state_ref, parts(g_ref, aux_ref), scaled_ref, stat_ref, aux_ref.shape[2])
    announce(stat_ref, message_ref)


def update(element_total, gathered_ref, state_ref, table_ref):
    spread(gathered_ref[...], table_ref)
    duals = [state_ref[i : i + 1, :] for i in range(N)]
    targets = [state_ref[TARGET_AT + i : TARGET_AT + i + 1, :] for i in range(N)]
    targets[-1] = targets[-1] + table_ref[VOL_AT : VOL_AT + 1, :] * (1.0 / element_total)
    return newton(table_ref, duals, targets, element_total), targets


def advance(element_total, gathered_ref, state_ref, new_state_ref, stat_ref, table_ref):
    duals, targets = update(element_total, gathered_ref, state_ref, table_ref)
    new_state_ref[...] = state_ref[...]
    for i in range(N):
        new_state_ref[i : i + 1, :] = duals[i]
    new_state_ref[TARGET_AT + N - 1 : TARGET_AT + N, :] = targets[-1]
    stat_ref[VOL_AT:, :] = jnp.zeros((STATS - VOL_AT, LANES), jnp.float32)


def middle_kernel(
    element_total,
    gathered_ref, state_ref, g_ref, aux_ref,
    new_state_ref, message_ref,
    scaled_ref, stat_ref, table_ref,
):
    advance(element_total, gathered_ref, state_ref, new_state_ref, stat_ref, table_ref)
    evaluate(new_state_ref, parts(g_ref, aux_ref), scaled_ref, stat_ref, aux_ref.shape[2])
    announce(stat_ref, message_ref)


def last_kernel(
    element_total,
    gathered_ref, state_ref, g_ref, aux_ref, x_ref,
    design_ref, duals_ref,
    table_ref,
):
    duals, _ = update(element_total, gathered_ref, state_ref, table_ref)
    lane = lax.broadcasted_iota(jnp.int32, (1, LANES), 1)
    row = jnp.zeros((1, LANES), jnp.float32)
    for i in range(N):
        row = jnp.where(lane == i, duals[i], row)
    duals_ref[...] = row[:, : duals_ref.shape[1]]
    depth = x_ref.shape[0]
    wide = [jnp.broadcast_to(l, (depth, LANES)) for l in duals]
    slopes, (a, b, lo, hi) = read(parts(g_ref, aux_ref), 0, pl.ds(0, depth))
    _, _, _, t = place(wide, slopes, a, b, lo, hi)
    design_ref[...] = x_ref[...] + t


def f32(*shape):
    return jax.ShapeDtypeStruct(shape, jnp.float32)


PARAMS = pltpu.CompilerParams(vmem_limit_bytes=16 * 1024 * 1024)
ORDER = ((("core", "x", "y"), ("z",)),) * (NEWTON - 1) + ((("core", "z"), ("x", "y")),)


def scratch(blocks, depth):
    return [
        pltpu.VMEM((N, blocks * depth, LANES), jnp.float32),
        pltpu.VMEM((STATS, LANES), jnp.float32),
        pltpu.VMEM((STATS, LANES), jnp.float32),
    ]


def per_device(sensitivity, x, x1, x2, gl, gu, w, case_values, duals_start):
    sizes = {name: lax.axis_size(name) for name in ("x", "core", "y", "z")}
    devices = sizes["x"] * sizes["core"] * sizes["y"] * sizes["z"]
    cases = sizes["x"] * sizes["core"]
    depth = x.size // LANES
    element_total = float(x.size * devices)
    shape = x.shape
    x, x1, x2, gl, gu, w = (v.reshape(depth, LANES) for v in (x, x1, x2, gl, gu, w))
    g = lax.all_to_all(
        sensitivity.reshape(cases, depth, LANES), ("x", "core"), split_axis=0, concat_axis=0, tiled=True
    ).reshape(1, cases, depth, LANES)

    def exchange(message, axes):
        return lax.all_to_all(message, axes, split_axis=0, concat_axis=0, tiled=True)

    def count_of(axes):
        return functools.reduce(lambda n, name: n * sizes[name], axes, 1)

    def gather(message, order):
        first, second = order
        part = jnp.sum(exchange(message, first), 0, keepdims=True)
        return exchange(jnp.broadcast_to(part, (count_of(second), LANES)), second)

    lower, upper, aux, volume, state = pl.pallas_call(
        prepare_kernel,
        out_shape=(
            f32(depth, LANES), f32(depth, LANES), f32(1, 5, depth, LANES), f32(8, LANES), f32(STATE, LANES),
        ),
        in_specs=[vmem()] * 8,
        out_specs=(vmem(),) * 5,
        compiler_params=PARAMS,
        cost_estimate=pl.CostEstimate(flops=10_000_000_000, bytes_accessed=40_000_000, transcendentals=0),
    )(duals_start.reshape(1, -1), case_values.reshape(1, -1), x, x1, x2, gl, gu, w)
    message = pl.pallas_call(
        first_kernel,
        out_shape=f32(count_of(ORDER[0][0]), LANES),
        in_specs=[vmem()] * 4,
        out_specs=vmem(),
        scratch_shapes=scratch(1, depth)[:2],
        compiler_params=PARAMS,
    )(g, aux, volume, state)
    for step in range(1, NEWTON):
        state, message = pl.pallas_call(
            functools.partial(middle_kernel, element_total),
            out_shape=(f32(STATE, LANES), f32(count_of(ORDER[step][0]), LANES)),
            in_specs=[vmem()] * 4,
            out_specs=(vmem(),) * 2,
            scratch_shapes=scratch(1, depth),
            compiler_params=PARAMS,
        )(gather(message, ORDER[step - 1]), state, g, aux)
    design, duals = pl.pallas_call(
        functools.partial(last_kernel, element_total),
        out_shape=(f32(depth, LANES), f32(1, N)),
        in_specs=[vmem()] * 5,
        out_specs=(vmem(),) * 2,
        scratch_shapes=scratch(1, depth)[2:],
        compiler_params=PARAMS,
    )(gather(message, ORDER[-1]), state, g, aux, x)
    return design.reshape(shape), lower.reshape(shape), upper.reshape(shape), duals.reshape(N)


def solution(mesh):
    cases, slabs = mesh.devices.shape
    fine = Mesh(mesh.devices.reshape(cases // 2, 2, 4, slabs // 4), ("x", "core", "y", "z"))
    case, slab = ("x", "core"), ("y", "z")
    design = P(slab, case, None)
    return jax.shard_map(
        per_device,
        mesh=fine,
        in_specs=(P(case, slab),) + (design,) * 6 + (P(), P()),
        out_specs=(design, design, design, P()),
        check_vma=False,
    )
```

```python
import functools

import jax
import jax.numpy as jnp
from jax import lax
from jax.experimental import pallas as pl
from jax.experimental.pallas import tpu as pltpu
from jax.sharding import Mesh
from jax.sharding import PartitionSpec as P

NEWTON = 4
PROX = 0.1
VOLFRAC = 0.4
N = 9
PAIRS = [(i, k) for i in range(N) for k in range(i + 1)]
GRAD_AT = len(PAIRS)
VOL_AT = GRAD_AT + N
LANES = 128
TARGET_AT = 16
STATE = 32
STATS = 64
CHUNK = 128
KUNROLL = 16
ORDER = ("nf", "nf", "nf", "fn")


def vmem():
    return pl.BlockSpec(memory_space=pltpu.VMEM)


def total(rows):
    while rows.shape[0] > 8:
        half = rows.shape[0] // 2
        rows = rows[:half] + rows[half:]
    return jnp.sum(rows, 0, keepdims=True)


def diagonal(values, count):
    row = lax.broadcasted_iota(jnp.int32, (count, LANES), 0)
    lane = lax.broadcasted_iota(jnp.int32, (count, LANES), 1)
    return jnp.where(row == lane, values, 0.0)


def spread(gathered, table_ref):
    sums = jnp.sum(diagonal(total(gathered), table_ref.shape[0]), 1, keepdims=True)
    table_ref[...] = jnp.broadcast_to(sums, table_ref.shape)


def solve(matrix, vector):
    m = dict(matrix)
    b = list(vector)
    inverse = []
    for k in range(N):
        r = 1.0 / m[k, k]
        inverse.append(r)
        for i in range(k + 1, N):
            scaled = m[i, k] * r
            for j in range(k + 1, i + 1):
                m[i, j] = m[i, j] - scaled * m[j, k]
            b[i] = b[i] - scaled * b[k]
    x = [None] * N
    for k in reversed(range(N)):
        running = b[k]
        for i in range(k + 1, N):
            running = running - m[i, k] * x[i]
        x[k] = running * inverse[k]
    return x


def newton(table_ref, duals, targets, element_total):
    scale = 1.0 / element_total
    excess = functools.reduce(jnp.add, duals[:-1]) - 1.0
    height = jnp.maximum(excess, 0.0)
    active = jnp.where(excess > 0, 1.0, 0.0)
    matrix = {}
    for at, (i, k) in enumerate(PAIRS):
        entry = table_ref[at : at + 1, :] * scale
        if i < N - 1:
            entry = entry + active
        matrix[i, k] = entry
    trace = functools.reduce(jnp.add, [matrix[i, i] for i in range(N)])
    damping = trace * (0.5 / N) + 0.0001
    vector = []
    for i in range(N):
        matrix[i, i] = matrix[i, i] + damping
        entry = table_ref[GRAD_AT + i : GRAD_AT + i + 1, :] * scale + targets[i]
        vector.append(entry - height if i < N - 1 else entry)
    step = solve(matrix, vector)
    return [jnp.maximum(l + d, 0.1 * l) for l, d in zip(duals, step)]


def place(duals, slopes, a, b, lo, hi):
    terms = [l * g for l, g in zip(duals, slopes)]
    rise = functools.reduce(jnp.add, [jnp.maximum(m, 0.0) for m in terms])
    fall = functools.reduce(jnp.add, [jnp.minimum(m, 0.0) for m in terms])
    p = PROX + (1.001 * rise - 0.001 * fall)
    q = PROX + (0.001 * rise - 1.001 * fall)
    root_p = p * lax.rsqrt(p)
    root_q = q * lax.rsqrt(q)
    free = a * b * (root_q - root_p) / (a * root_p + b * root_q)
    return p, q, free, jnp.minimum(jnp.maximum(free, lo), hi)


def parts(g_ref, aux_ref):
    return lambda block, k, rows: g_ref[block, k, rows, :] if k < N - 1 else aux_ref[block, k - N + 1, rows, :]


def read(part, block, rows):
    held = [part(block, k, rows) for k in range(N + 4)]
    return held[:N], held[N:]


def evaluate(state_ref, part, scaled_ref, stat_ref, depth):
    blocks = scaled_ref.shape[1] // depth

    def fold(v):
        return jnp.sum(v.reshape(-1, 8, LANES), 0)

    def column(j, grads):
        at = pl.multiple_of(j * CHUNK, CHUNK)
        block = j // (depth // CHUNK)
        rows = pl.ds(pl.multiple_of(at - block * depth, CHUNK), CHUNK)
        slopes, (a, b, lo, hi) = read(part, block, rows)
        duals = [jnp.broadcast_to(state_ref[i : i + 1, :], (CHUNK, LANES)) for i in range(N)]
        p, q, free, t = place(duals, slopes, a, b, lo, hi)
        inside = (free > lo) & (free < hi)
        to_upper = a - t
        to_lower = b + t
        both = 1.0 / (to_upper * to_lower)
        ru = both * to_lower
        rl = both * to_upper
        up_at = a * ru
        down_at = b * rl
        up_two = up_at * up_at
        down_two = down_at * down_at
        curve = 2.0 * (p * up_two * ru + q * down_two * rl)
        root = jnp.where(inside, lax.rsqrt(curve), 0.0)
        cu, cd = up_two * root, down_two * root
        tu, td = t * up_at, t * down_at
        c_rise, c_fall = 1.001 * cu - 0.001 * cd, 1.001 * cd - 0.001 * cu
        t_rise, t_fall = 1.001 * tu - 0.001 * td, 1.001 * td - 0.001 * tu
        out = []
        for i, g in enumerate(slopes):
            rising = g > 0
            scaled_ref[i, pl.ds(at, CHUNK), :] = g * jnp.where(rising, c_rise, c_fall)
            out.append(grads[i] + fold(g * jnp.where(rising, t_rise, t_fall)))
        return tuple(out)

    zero = jnp.zeros((8, LANES), jnp.float32)
    steps = blocks * depth // CHUNK
    grads = lax.fori_loop(0, steps, column, (zero,) * N) if steps > 1 else column(0, (zero,) * N)
    for i in range(N):
        stat_ref[GRAD_AT + i : GRAD_AT + i + 1, :] = jnp.sum(grads[i], 0, keepdims=True)
    groups = [(0, 5), (5, 9)]
    for at, (i0, i1) in enumerate(groups):
        for k0, k1 in groups[: at + 1]:
            pairs = [(i, k) for i in range(i0, i1) for k in range(k0, min(k1, i + 1))]

            def products(j, sums, pairs=pairs):
                rows = pl.ds(pl.multiple_of(j * 8, 8), 8)
                held = {i: scaled_ref[i, rows, :] for i in sorted({i for pair in pairs for i in pair})}
                return tuple(s + held[i] * held[k] for s, (i, k) in zip(sums, pairs))

            sums = lax.fori_loop(0, blocks * depth // 8, products, (zero,) * len(pairs), unroll=KUNROLL)
            for s, pair in zip(sums, pairs):
                row = PAIRS.index(pair)
                stat_ref[row : row + 1, :] = jnp.sum(s, 0, keepdims=True)


def announce(stat_ref, message_ref):
    sums = jnp.sum(stat_ref[...], 1, keepdims=True)
    sums = total(diagonal(sums, stat_ref.shape[0]))
    message_ref[...] = jnp.broadcast_to(sums, message_ref.shape)


def prepare_kernel(
    duals_ref, case_values_ref, x_ref, x1_ref, x2_ref, gl_ref, gu_ref, w_ref,
    lower_ref, upper_ref, aux_ref, volume_ref, state_ref,
):
    x, x1, x2, w = (r[...] for r in (x_ref, x1_ref, x2_ref, w_ref))
    trend = (x - x1) * (x1 - x2)
    factor = jnp.where(trend > 0, 1.2, jnp.where(trend < 0, 0.7, 1.0))
    lower = jnp.minimum(x - factor * gl_ref[...], x - 0.01)
    upper = jnp.maximum(x + factor * gu_ref[...], x + 0.01)
    lower_ref[...] = lower
    upper_ref[...] = upper
    a = upper - x
    b = x - lower
    aux_ref[0, 0] = w
    aux_ref[0, 1] = a
    aux_ref[0, 2] = b
    aux_ref[0, 3] = jnp.maximum(jnp.maximum(lower + 0.1 * b, x - 0.2), 0.0) - x
    aux_ref[0, 4] = jnp.minimum(jnp.minimum(upper - 0.1 * a, x + 0.2), 1.0) - x
    volume_ref[...] = jnp.sum((w * x).reshape(-1, 8, LANES), 0)
    state_ref[...] = jnp.zeros(state_ref.shape, jnp.float32)
    for i in range(N):
        state_ref[i : i + 1, :] = jnp.broadcast_to(duals_ref[0:1, i : i + 1], (1, LANES))
    for i in range(N - 1):
        state_ref[TARGET_AT + i : TARGET_AT + i + 1, :] = jnp.broadcast_to(
            case_values_ref[0:1, i : i + 1], (1, LANES)
        )
    state_ref[TARGET_AT + N - 1 : TARGET_AT + N, :] = jnp.full((1, LANES), -VOLFRAC)


def first_kernel(g_ref, aux_ref, volume_ref, state_ref, message_ref, scaled_ref, stat_ref):
    stat_ref[VOL_AT:, :] = jnp.zeros((STATS - VOL_AT, LANES), jnp.float32)
    stat_ref[VOL_AT : VOL_AT + 1, :] = jnp.sum(volume_ref[...], 0, keepdims=True)
    evaluate(state_ref, parts(g_ref, aux_ref), scaled_ref, stat_ref, aux_ref.shape[2])
    announce(stat_ref, message_ref)


def update(element_total, gathered_ref, state_ref, table_ref):
    spread(gathered_ref[...], table_ref)
    duals = [state_ref[i : i + 1, :] for i in range(N)]
    targets = [state_ref[TARGET_AT + i : TARGET_AT + i + 1, :] for i in range(N)]
    targets[-1] = targets[-1] + table_ref[VOL_AT : VOL_AT + 1, :] * (1.0 / element_total)
    return newton(table_ref, duals, targets, element_total), targets


def advance(element_total, gathered_ref, state_ref, new_state_ref, stat_ref, table_ref):
    duals, targets = update(element_total, gathered_ref, state_ref, table_ref)
    new_state_ref[...] = state_ref[...]
    for i in range(N):
        new_state_ref[i : i + 1, :] = duals[i]
    new_state_ref[TARGET_AT + N - 1 : TARGET_AT + N, :] = targets[-1]
    stat_ref[VOL_AT:, :] = jnp.zeros((STATS - VOL_AT, LANES), jnp.float32)


def middle_kernel(
    element_total,
    gathered_ref, state_ref, g_ref, aux_ref,
    new_state_ref, message_ref,
    scaled_ref, stat_ref, table_ref,
):
    advance(element_total, gathered_ref, state_ref, new_state_ref, stat_ref, table_ref)
    evaluate(new_state_ref, parts(g_ref, aux_ref), scaled_ref, stat_ref, aux_ref.shape[2])
    announce(stat_ref, message_ref)


def last_kernel(
    element_total,
    gathered_ref, state_ref, g_ref, aux_ref, x_ref,
    design_ref, duals_ref,
    table_ref,
):
    duals, _ = update(element_total, gathered_ref, state_ref, table_ref)
    lane = lax.broadcasted_iota(jnp.int32, (1, LANES), 1)
    row = jnp.zeros((1, LANES), jnp.float32)
    for i in range(N):
        row = jnp.where(lane == i, duals[i], row)
    duals_ref[...] = row[:, : duals_ref.shape[1]]
    depth = x_ref.shape[0]
    wide = [jnp.broadcast_to(l, (depth, LANES)) for l in duals]
    slopes, (a, b, lo, hi) = read(parts(g_ref, aux_ref), 0, pl.ds(0, depth))
    _, _, _, t = place(wide, slopes, a, b, lo, hi)
    design_ref[...] = x_ref[...] + t


def f32(*shape):
    return jax.ShapeDtypeStruct(shape, jnp.float32)


PARAMS = pltpu.CompilerParams(vmem_limit_bytes=16 * 1024 * 1024)
NEAR = ("y", "x")
FAR = ("core", "z")


def scratch(blocks, depth):
    return [
        pltpu.VMEM((N, blocks * depth, LANES), jnp.float32),
        pltpu.VMEM((STATS, LANES), jnp.float32),
        pltpu.VMEM((STATS, LANES), jnp.float32),
    ]


def per_device(sensitivity, x, x1, x2, gl, gu, w, case_values, duals_start):
    sizes = {name: lax.axis_size(name) for name in ("x", "core", "y", "z")}
    near = sizes["x"] * sizes["y"]
    far = sizes["core"] * sizes["z"]
    cases = sizes["x"] * sizes["core"]
    depth = x.size // LANES
    element_total = float(x.size * near * far)
    shape = x.shape
    x, x1, x2, gl, gu, w = (v.reshape(depth, LANES) for v in (x, x1, x2, gl, gu, w))
    g = lax.all_to_all(
        sensitivity.reshape(cases, depth, LANES), ("x", "core"), split_axis=0, concat_axis=0, tiled=True
    ).reshape(1, cases, depth, LANES)

    def exchange(message, axes):
        return lax.all_to_all(message, axes, split_axis=0, concat_axis=0, tiled=True)

    stages = {"n": (NEAR, near), "f": (FAR, far)}

    def gather(message, order):
        (first, _), (second, count) = (stages[name] for name in order)
        part = jnp.sum(exchange(message, first), 0, keepdims=True)
        return exchange(jnp.broadcast_to(part, (count, LANES)), second)

    lower, upper, aux, volume, state = pl.pallas_call(
        prepare_kernel,
        out_shape=(
            f32(depth, LANES), f32(depth, LANES), f32(1, 5, depth, LANES), f32(8, LANES), f32(STATE, LANES),
        ),
        in_specs=[vmem()] * 8,
        out_specs=(vmem(),) * 5,
        compiler_params=PARAMS,
        cost_estimate=pl.CostEstimate(flops=10_000_000_000, bytes_accessed=40_000_000, transcendentals=0),
    )(duals_start.reshape(1, -1), case_values.reshape(1, -1), x, x1, x2, gl, gu, w)
    message = pl.pallas_call(
        first_kernel,
        out_shape=f32(stages[ORDER[0][0]][1], LANES),
        in_specs=[vmem()] * 4,
        out_specs=vmem(),
        scratch_shapes=scratch(1, depth)[:2],
        compiler_params=PARAMS,
    )(g, aux, volume, state)
    for step in range(1, NEWTON):
        state, message = pl.pallas_call(
            functools.partial(middle_kernel, element_total),
            out_shape=(f32(STATE, LANES), f32(stages[ORDER[step][0]][1], LANES)),
            in_specs=[vmem()] * 4,
            out_specs=(vmem(),) * 2,
            scratch_shapes=scratch(1, depth),
            compiler_params=PARAMS,
        )(gather(message, ORDER[step - 1]), state, g, aux)
    design, duals = pl.pallas_call(
        functools.partial(last_kernel, element_total),
        out_shape=(f32(depth, LANES), f32(1, N)),
        in_specs=[vmem()] * 5,
        out_specs=(vmem(),) * 2,
        scratch_shapes=scratch(1, depth)[2:],
        compiler_params=PARAMS,
    )(gather(message, ORDER[-1]), state, g, aux, x)
    return design.reshape(shape), lower.reshape(shape), upper.reshape(shape), duals.reshape(N)


def solution(mesh):
    cases, slabs = mesh.devices.shape
    fine = Mesh(mesh.devices.reshape(cases // 2, 2, 4, slabs // 4), ("x", "core", "y", "z"))
    case, slab = ("x", "core"), ("y", "z")
    design = P(slab, case, None)
    return jax.shard_map(
        per_device,
        mesh=fine,
        in_specs=(P(case, slab),) + (design,) * 6 + (P(), P()),
        out_specs=(design, design, design, P()),
        check_vma=False,
    )
```

```python
import functools

import jax
import jax.numpy as jnp
from jax import lax
from jax.experimental import pallas as pl
from jax.experimental.pallas import tpu as pltpu
from jax.sharding import Mesh
from jax.sharding import PartitionSpec as P

NEWTON = 4
PROX = 0.1
VOLFRAC = 0.4
N = 9
PAIRS = [(i, k) for i in range(N) for k in range(i + 1)]
GRAD_AT = len(PAIRS)
VOL_AT = GRAD_AT + N
LANES = 128
TARGET_AT = 16
STATE = 32
STATS = 64
CHUNK = 128
KUNROLL = 16
ORDER = ("nf", "nf", "nf", "pz")


def vmem():
    return pl.BlockSpec(memory_space=pltpu.VMEM)


def total(rows):
    while rows.shape[0] > 8:
        half = rows.shape[0] // 2
        rows = rows[:half] + rows[half:]
    return jnp.sum(rows, 0, keepdims=True)


def diagonal(values, count):
    row = lax.broadcasted_iota(jnp.int32, (count, LANES), 0)
    lane = lax.broadcasted_iota(jnp.int32, (count, LANES), 1)
    return jnp.where(row == lane, values, 0.0)


def spread(gathered, table_ref):
    sums = jnp.sum(diagonal(total(gathered), table_ref.shape[0]), 1, keepdims=True)
    table_ref[...] = jnp.broadcast_to(sums, table_ref.shape)


def solve(matrix, vector):
    m = dict(matrix)
    b = list(vector)
    inverse = []
    for k in range(N):
        r = 1.0 / m[k, k]
        inverse.append(r)
        for i in range(k + 1, N):
            scaled = m[i, k] * r
            for j in range(k + 1, i + 1):
                m[i, j] = m[i, j] - scaled * m[j, k]
            b[i] = b[i] - scaled * b[k]
    x = [None] * N
    for k in reversed(range(N)):
        running = b[k]
        for i in range(k + 1, N):
            running = running - m[i, k] * x[i]
        x[k] = running * inverse[k]
    return x


def newton(table_ref, duals, targets, element_total):
    scale = 1.0 / element_total
    excess = functools.reduce(jnp.add, duals[:-1]) - 1.0
    height = jnp.maximum(excess, 0.0)
    active = jnp.where(excess > 0, 1.0, 0.0)
    matrix = {}
    for at, (i, k) in enumerate(PAIRS):
        entry = table_ref[at : at + 1, :] * scale
        if i < N - 1:
            entry = entry + active
        matrix[i, k] = entry
    trace = functools.reduce(jnp.add, [matrix[i, i] for i in range(N)])
    damping = trace * (0.5 / N) + 0.0001
    vector = []
    for i in range(N):
        matrix[i, i] = matrix[i, i] + damping
        entry = table_ref[GRAD_AT + i : GRAD_AT + i + 1, :] * scale + targets[i]
        vector.append(entry - height if i < N - 1 else entry)
    step = solve(matrix, vector)
    return [jnp.maximum(l + d, 0.1 * l) for l, d in zip(duals, step)]


def place(duals, slopes, a, b, lo, hi):
    terms = [l * g for l, g in zip(duals, slopes)]
    rise = functools.reduce(jnp.add, [jnp.maximum(m, 0.0) for m in terms])
    fall = functools.reduce(jnp.add, [jnp.minimum(m, 0.0) for m in terms])
    p = PROX + (1.001 * rise - 0.001 * fall)
    q = PROX + (0.001 * rise - 1.001 * fall)
    root_p = p * lax.rsqrt(p)
    root_q = q * lax.rsqrt(q)
    free = a * b * (root_q - root_p) / (a * root_p + b * root_q)
    return p, q, free, jnp.minimum(jnp.maximum(free, lo), hi)


def parts(g_ref, aux_ref):
    return lambda block, k, rows: g_ref[block, k, rows, :] if k < N - 1 else aux_ref[block, k - N + 1, rows, :]


def read(part, block, rows):
    held = [part(block, k, rows) for k in range(N + 4)]
    return held[:N], held[N:]


def evaluate(state_ref, part, scaled_ref, stat_ref, depth):
    blocks = scaled_ref.shape[1] // depth

    def fold(v):
        return jnp.sum(v.reshape(-1, 8, LANES), 0)

    def column(j, grads):
        at = pl.multiple_of(j * CHUNK, CHUNK)
        block = j // (depth // CHUNK)
        rows = pl.ds(pl.multiple_of(at - block * depth, CHUNK), CHUNK)
        slopes, (a, b, lo, hi) = read(part, block, rows)
        duals = [jnp.broadcast_to(state_ref[i : i + 1, :], (CHUNK, LANES)) for i in range(N)]
        p, q, free, t = place(duals, slopes, a, b, lo, hi)
        inside = (free > lo) & (free < hi)
        to_upper = a - t
        to_lower = b + t
        both = 1.0 / (to_upper * to_lower)
        ru = both * to_lower
        rl = both * to_upper
        up_at = a * ru
        down_at = b * rl
        up_two = up_at * up_at
        down_two = down_at * down_at
        curve = 2.0 * (p * up_two * ru + q * down_two * rl)
        root = jnp.where(inside, lax.rsqrt(curve), 0.0)
        cu, cd = up_two * root, down_two * root
        tu, td = t * up_at, t * down_at
        c_rise, c_fall = 1.001 * cu - 0.001 * cd, 1.001 * cd - 0.001 * cu
        t_rise, t_fall = 1.001 * tu - 0.001 * td, 1.001 * td - 0.001 * tu
        out = []
        for i, g in enumerate(slopes):
            rising = g > 0
            scaled_ref[i, pl.ds(at, CHUNK), :] = g * jnp.where(rising, c_rise, c_fall)
            out.append(grads[i] + fold(g * jnp.where(rising, t_rise, t_fall)))
        return tuple(out)

    zero = jnp.zeros((8, LANES), jnp.float32)
    steps = blocks * depth // CHUNK
    grads = lax.fori_loop(0, steps, column, (zero,) * N) if steps > 1 else column(0, (zero,) * N)
    for i in range(N):
        stat_ref[GRAD_AT + i : GRAD_AT + i + 1, :] = jnp.sum(grads[i], 0, keepdims=True)
    groups = [(0, 5), (5, 9)]
    for at, (i0, i1) in enumerate(groups):
        for k0, k1 in groups[: at + 1]:
            pairs = [(i, k) for i in range(i0, i1) for k in range(k0, min(k1, i + 1))]

            def products(j, sums, pairs=pairs):
                rows = pl.ds(pl.multiple_of(j * 8, 8), 8)
                held = {i: scaled_ref[i, rows, :] for i in sorted({i for pair in pairs for i in pair})}
                return tuple(s + held[i] * held[k] for s, (i, k) in zip(sums, pairs))

            sums = lax.fori_loop(0, blocks * depth // 8, products, (zero,) * len(pairs), unroll=KUNROLL)
            for s, pair in zip(sums, pairs):
                row = PAIRS.index(pair)
                stat_ref[row : row + 1, :] = jnp.sum(s, 0, keepdims=True)


def announce(stat_ref, message_ref):
    sums = jnp.sum(stat_ref[...], 1, keepdims=True)
    sums = total(diagonal(sums, stat_ref.shape[0]))
    message_ref[...] = jnp.broadcast_to(sums, message_ref.shape)


def prepare_kernel(
    duals_ref, case_values_ref, x_ref, x1_ref, x2_ref, gl_ref, gu_ref, w_ref,
    lower_ref, upper_ref, aux_ref, volume_ref, state_ref,
):
    x, x1, x2, w = (r[...] for r in (x_ref, x1_ref, x2_ref, w_ref))
    trend = (x - x1) * (x1 - x2)
    factor = jnp.where(trend > 0, 1.2, jnp.where(trend < 0, 0.7, 1.0))
    lower = jnp.minimum(x - factor * gl_ref[...], x - 0.01)
    upper = jnp.maximum(x + factor * gu_ref[...], x + 0.01)
    lower_ref[...] = lower
    upper_ref[...] = upper
    a = upper - x
    b = x - lower
    aux_ref[0, 0] = w
    aux_ref[0, 1] = a
    aux_ref[0, 2] = b
    aux_ref[0, 3] = jnp.maximum(jnp.maximum(lower + 0.1 * b, x - 0.2), 0.0) - x
    aux_ref[0, 4] = jnp.minimum(jnp.minimum(upper - 0.1 * a, x + 0.2), 1.0) - x
    volume_ref[...] = jnp.sum((w * x).reshape(-1, 8, LANES), 0)
    state_ref[...] = jnp.zeros(state_ref.shape, jnp.float32)
    for i in range(N):
        state_ref[i : i + 1, :] = jnp.broadcast_to(duals_ref[0:1, i : i + 1], (1, LANES))
    for i in range(N - 1):
        state_ref[TARGET_AT + i : TARGET_AT + i + 1, :] = jnp.broadcast_to(
            case_values_ref[0:1, i : i + 1], (1, LANES)
        )
    state_ref[TARGET_AT + N - 1 : TARGET_AT + N, :] = jnp.full((1, LANES), -VOLFRAC)


def first_kernel(g_ref, aux_ref, volume_ref, state_ref, message_ref, scaled_ref, stat_ref):
    stat_ref[VOL_AT:, :] = jnp.zeros((STATS - VOL_AT, LANES), jnp.float32)
    stat_ref[VOL_AT : VOL_AT + 1, :] = jnp.sum(volume_ref[...], 0, keepdims=True)
    evaluate(state_ref, parts(g_ref, aux_ref), scaled_ref, stat_ref, aux_ref.shape[2])
    announce(stat_ref, message_ref)


def update(element_total, gathered_ref, state_ref, table_ref):
    spread(gathered_ref[...], table_ref)
    duals = [state_ref[i : i + 1, :] for i in range(N)]
    targets = [state_ref[TARGET_AT + i : TARGET_AT + i + 1, :] for i in range(N)]
    targets[-1] = targets[-1] + table_ref[VOL_AT : VOL_AT + 1, :] * (1.0 / element_total)
    return newton(table_ref, duals, targets, element_total), targets


def advance(element_total, gathered_ref, state_ref, new_state_ref, stat_ref, table_ref):
    duals, targets = update(element_total, gathered_ref, state_ref, table_ref)
    new_state_ref[...] = state_ref[...]
    for i in range(N):
        new_state_ref[i : i + 1, :] = duals[i]
    new_state_ref[TARGET_AT + N - 1 : TARGET_AT + N, :] = targets[-1]
    stat_ref[VOL_AT:, :] = jnp.zeros((STATS - VOL_AT, LANES), jnp.float32)


def middle_kernel(
    element_total,
    gathered_ref, state_ref, g_ref, aux_ref,
    new_state_ref, message_ref,
    scaled_ref, stat_ref, table_ref,
):
    advance(element_total, gathered_ref, state_ref, new_state_ref, stat_ref, table_ref)
    evaluate(new_state_ref, parts(g_ref, aux_ref), scaled_ref, stat_ref, aux_ref.shape[2])
    announce(stat_ref, message_ref)


def last_kernel(
    element_total,
    gathered_ref, state_ref, g_ref, aux_ref, x_ref,
    design_ref, duals_ref,
    table_ref,
):
    duals, _ = update(element_total, gathered_ref, state_ref, table_ref)
    lane = lax.broadcasted_iota(jnp.int32, (1, LANES), 1)
    row = jnp.zeros((1, LANES), jnp.float32)
    for i in range(N):
        row = jnp.where(lane == i, duals[i], row)
    duals_ref[...] = row[:, : duals_ref.shape[1]]
    depth = x_ref.shape[0]
    wide = [jnp.broadcast_to(l, (depth, LANES)) for l in duals]
    slopes, (a, b, lo, hi) = read(parts(g_ref, aux_ref), 0, pl.ds(0, depth))
    _, _, _, t = place(wide, slopes, a, b, lo, hi)
    design_ref[...] = x_ref[...] + t


def f32(*shape):
    return jax.ShapeDtypeStruct(shape, jnp.float32)


PARAMS = pltpu.CompilerParams(vmem_limit_bytes=16 * 1024 * 1024)
NEAR = ("y", "x")
FAR = ("core", "z")


def scratch(blocks, depth):
    return [
        pltpu.VMEM((N, blocks * depth, LANES), jnp.float32),
        pltpu.VMEM((STATS, LANES), jnp.float32),
        pltpu.VMEM((STATS, LANES), jnp.float32),
    ]


def per_device(sensitivity, x, x1, x2, gl, gu, w, case_values, duals_start):
    sizes = {name: lax.axis_size(name) for name in ("x", "core", "y", "z")}
    near = sizes["x"] * sizes["y"]
    far = sizes["core"] * sizes["z"]
    cases = sizes["x"] * sizes["core"]
    depth = x.size // LANES
    element_total = float(x.size * near * far)
    shape = x.shape
    x, x1, x2, gl, gu, w = (v.reshape(depth, LANES) for v in (x, x1, x2, gl, gu, w))
    g = lax.all_to_all(
        sensitivity.reshape(cases, depth, LANES), ("x", "core"), split_axis=0, concat_axis=0, tiled=True
    ).reshape(1, cases, depth, LANES)

    def exchange(message, axes):
        return lax.all_to_all(message, axes, split_axis=0, concat_axis=0, tiled=True)

    stages = {"n": (NEAR, near), "f": (FAR, far), "p": (("core",) + NEAR, sizes["core"] * near), "z": (("z",), sizes["z"])}

    def gather(message, order):
        (first, _), (second, count) = (stages[name] for name in order)
        part = jnp.sum(exchange(message, first), 0, keepdims=True)
        return exchange(jnp.broadcast_to(part, (count, LANES)), second)

    lower, upper, aux, volume, state = pl.pallas_call(
        prepare_kernel,
        out_shape=(
            f32(depth, LANES), f32(depth, LANES), f32(1, 5, depth, LANES), f32(8, LANES), f32(STATE, LANES),
        ),
        in_specs=[vmem()] * 8,
        out_specs=(vmem(),) * 5,
        compiler_params=PARAMS,
        cost_estimate=pl.CostEstimate(flops=10_000_000_000, bytes_accessed=40_000_000, transcendentals=0),
    )(duals_start.reshape(1, -1), case_values.reshape(1, -1), x, x1, x2, gl, gu, w)
    message = pl.pallas_call(
        first_kernel,
        out_shape=f32(stages[ORDER[0][0]][1], LANES),
        in_specs=[vmem()] * 4,
        out_specs=vmem(),
        scratch_shapes=scratch(1, depth)[:2],
        compiler_params=PARAMS,
    )(g, aux, volume, state)
    for step in range(1, NEWTON):
        state, message = pl.pallas_call(
            functools.partial(middle_kernel, element_total),
            out_shape=(f32(STATE, LANES), f32(stages[ORDER[step][0]][1], LANES)),
            in_specs=[vmem()] * 4,
            out_specs=(vmem(),) * 2,
            scratch_shapes=scratch(1, depth),
            compiler_params=PARAMS,
        )(gather(message, ORDER[step - 1]), state, g, aux)
    design, duals = pl.pallas_call(
        functools.partial(last_kernel, element_total),
        out_shape=(f32(depth, LANES), f32(1, N)),
        in_specs=[vmem()] * 5,
        out_specs=(vmem(),) * 2,
        scratch_shapes=scratch(1, depth)[2:],
        compiler_params=PARAMS,
    )(gather(message, ORDER[-1]), state, g, aux, x)
    return design.reshape(shape), lower.reshape(shape), upper.reshape(shape), duals.reshape(N)


def solution(mesh):
    cases, slabs = mesh.devices.shape
    fine = Mesh(mesh.devices.reshape(cases // 2, 2, 4, slabs // 4), ("x", "core", "y", "z"))
    case, slab = ("x", "core"), ("y", "z")
    design = P(slab, case, None)
    return jax.shard_map(
        per_device,
        mesh=fine,
        in_specs=(P(case, slab),) + (design,) * 6 + (P(), P()),
        out_specs=(design, design, design, P()),
        check_vma=False,
    )
```
